512 devices in a mesh: region: 64 (over z, y), depth: 8 (over x, core).
Axes of the slice: x: 4, y: 4, z: 16, core: 2. Of those that a mesh axis runs over, the one named last changes fastest.
Arguments:
- adjoint_seed: float32 [64, 16, 8192], P('depth', None, 'region'), may hold values from -6 to 6
- column_lengths: int32 [8192], P('region'), may hold values from 1 to 64
- lateral_tiles: bfloat16 [384, 8192, 128], P('depth', 'region'), may hold values from -0.0546875 to 0.0546875
- lateral_rows: int32 [384, 64], P('depth', 'region'), may hold values from 0 to 7
- lateral_sides: int32 [384, 64], P('depth', 'region'), may hold values from 0 to 2
- lateral_targets: int32 [384, 64], P('depth', 'region'), may hold values from 0 to 7
- lateral_counts: int32 [8, 64], P('depth', 'region'), may hold values from 12 to 48, as said below
- vertical_tiles: bfloat16 [128, 8192, 128], P('depth', 'region'), may hold values from -0.09375 to 0.09375
- vertical_rows: int32 [128, 64], P('depth', 'region'), may hold values from 0 to 7
- vertical_peers: int32 [128, 64], P('depth', 'region'), may hold values from 0 to 7
- vertical_targets: int32 [128, 64], P('depth', 'region'), may hold values from 0 to 7
Outputs:
- adjoint: float32 [64, 16, 8192], P('depth', None, 'region')
The draws below stay inside these ranges and needn't reach their ends.
Inputs may be any that keep to these rules, and one draw needn't show every extreme that they name: `lateral_counts`: some device uses all 48 slots in every draw.
All inputs are finite; a program needn't handle non-finite values.
Results may differ from the reference program's by a relative error of at most 0.0075.
Values may be sent and summed in bfloat16 or wider, within the bound.
No kernel may reach another device: no remote copies, remote signals or barrier semaphores. Data moves between devices by JAX's collectives and lax.ppermute only.
A program may use at most 64 MiB of HBM per device.

```python
import jax
import jax.numpy as jnp
from jax import lax

TRACERS = 16
TILE = 128
LEV_DEV = 8
LAT_SLOTS = 48
VERT_SLOTS = 16
STEPS = 12
LEVELS = 64
COLUMNS = 8192
N_REGION = 64
N_DEPTH = 8


def draw_lateral_counts(key, part):
    key = jax.random.fold_in(key, 7)
    counts = jax.random.randint(key, (N_DEPTH, N_REGION), LAT_SLOTS // 4, LAT_SLOTS + 1)
    return counts.at[0, 0].set(LAT_SLOTS).astype(jnp.int32)


def set_ends(result, stream_key, least, high):
    place = [jax.random.randint(jax.random.fold_in(stream_key, axis), (), 0, length) for axis, length in enumerate(result.shape)]
    main_axis = result.shape.index(max(result.shape))
    neighbour = place[:main_axis] + [(place[main_axis] + 1) % result.shape[main_axis]] + place[main_axis + 1:]
    return result.at[tuple(place)].set(least).at[tuple(neighbour)].set(high)


def block_levels(rng, shape, pieces, smallest, top_value):
    level, own = 1.0, jax.random.fold_in(rng, 6)
    for axis_at, shards_of in pieces:
        draws = jnp.exp(jax.random.uniform(jax.random.fold_in(own, axis_at), (shards_of,), jnp.float32, smallest / len(pieces), top_value / len(pieces)))
        level = level * jnp.repeat(draws, shape[axis_at] // shards_of).reshape([-1 if axis == axis_at else 1 for axis in range(len(shape))])
    return level


def normal_values(stream_key, shape, spread, most, cuts=(), kind=jnp.bfloat16):
    values = spread * jax.random.normal(stream_key, shape, jnp.float32)
    if cuts:
        values = values * block_levels(stream_key, shape, cuts, -0.22, 0.18)
    return jnp.clip(values, -most, most).astype(kind)


def setup_inputs(seed: int = 0) -> dict:
    key_list = jax.random.split(jax.random.key(seed), 12)
    return {
        "adjoint_seed": normal_values(key_list[0], (LEVELS, TRACERS, COLUMNS), 1.0, 6.0, ((0, 8), (2, 64)), jnp.float32),
        "column_lengths": set_ends(jax.random.randint(key_list[1], (COLUMNS,), 1, LEVELS + 1), jax.random.fold_in(key_list[1], 1), 1, LEVELS).astype(jnp.int32),
        "lateral_tiles": normal_values(key_list[2], (N_DEPTH * LAT_SLOTS, N_REGION * TILE, TILE), (16 * TILE * LAT_SLOTS // LEV_DEV) ** -0.5, 0.0546875, ((0, 8), (1, 64))),
        "lateral_rows": set_ends(jax.random.randint(key_list[3], (N_DEPTH * LAT_SLOTS, N_REGION), 0, LEV_DEV), jax.random.fold_in(key_list[3], 1), 0, LEV_DEV - 1).astype(jnp.int32),
        "lateral_sides": set_ends(jax.random.randint(key_list[4], (N_DEPTH * LAT_SLOTS, N_REGION), 0, 3), jax.random.fold_in(key_list[4], 1), 0, 2).astype(jnp.int32),
        "lateral_targets": set_ends(jax.random.randint(key_list[5], (N_DEPTH * LAT_SLOTS, N_REGION), 0, LEV_DEV), jax.random.fold_in(key_list[5], 1), 0, LEV_DEV - 1).astype(jnp.int32),
        "lateral_counts": draw_lateral_counts(jax.random.fold_in(key_list[11], 71), 0),
        "vertical_tiles": normal_values(key_list[7], (N_DEPTH * VERT_SLOTS, N_REGION * TILE, TILE), (16 * TILE * VERT_SLOTS // LEV_DEV) ** -0.5, 0.09375, ((0, 8), (1, 64))),
        "vertical_rows": set_ends(jax.random.randint(key_list[8], (N_DEPTH * VERT_SLOTS, N_REGION), 0, LEV_DEV), jax.random.fold_in(key_list[8], 1), 0, LEV_DEV - 1).astype(jnp.int32),
        "vertical_peers": set_ends(jax.random.randint(key_list[9], (N_DEPTH * VERT_SLOTS, N_REGION), 0, N_DEPTH), jax.random.fold_in(key_list[9], 1), 0, N_DEPTH - 1).astype(jnp.int32),
        "vertical_targets": set_ends(jax.random.randint(key_list[10], (N_DEPTH * VERT_SLOTS, N_REGION), 0, LEV_DEV), jax.random.fold_in(key_list[10], 1), 0, LEV_DEV - 1).astype(jnp.int32),
    }


def to_blocks(field):
    shaped = field.reshape(N_DEPTH, LEV_DEV, TRACERS, N_REGION, TILE)
    return shaped.transpose(3, 0, 1, 2, 4)


def from_blocks(blocks):
    return blocks.transpose(1, 2, 3, 0, 4).reshape(LEVELS, TRACERS, COLUMNS)


def slot_products(rounded_here, tile_here, row_here):
    picked = jnp.take_along_axis(rounded_here, row_here[:, :, None, None], axis=1).astype(jnp.float32)
    return jnp.einsum("dktc,dkce->dkte", picked, tile_here.astype(jnp.float32), precision=lax.Precision.HIGHEST)


def lateral_terms(blocks, tiles, rows, sides, targets, counts):
    rounded = blocks.astype(jnp.bfloat16)
    tile_all = tiles.reshape(N_DEPTH, LAT_SLOTS, N_REGION, TILE, TILE)
    row_all = rows.reshape(N_DEPTH, LAT_SLOTS, N_REGION)
    side_all = sides.reshape(N_DEPTH, LAT_SLOTS, N_REGION)
    target_all = targets.reshape(N_DEPTH, LAT_SLOTS, N_REGION)
    slot_ids = jnp.arange(LAT_SLOTS, dtype=jnp.int32)
    column_ids = jnp.arange(3 * LEV_DEV, dtype=jnp.int32)

    def visit(total, region):
        tile_here = lax.dynamic_index_in_dim(tile_all, region, 2, keepdims=False)
        row_here = lax.dynamic_index_in_dim(row_all, region, 2, keepdims=False)
        side_here = lax.dynamic_index_in_dim(side_all, region, 2, keepdims=False)
        target_here = lax.dynamic_index_in_dim(target_all, region, 2, keepdims=False)
        count_here = lax.dynamic_index_in_dim(counts, region, 1, keepdims=False)
        rounded_here = lax.dynamic_index_in_dim(rounded, region, 0, keepdims=False)
        product = slot_products(rounded_here, tile_here, row_here)
        in_use = slot_ids[None, :] < count_here[:, None]
        target = side_here * LEV_DEV + target_here
        placer = ((target[:, :, None] == column_ids[None, None, :]) & in_use[:, :, None]).astype(jnp.float32)
        partial_value = jnp.einsum("dkj,dkte->djte", placer, product, precision=lax.Precision.HIGHEST)
        partial_value = lax.optimization_barrier(partial_value.astype(jnp.bfloat16)).astype(jnp.float32)
        partial_value = partial_value.reshape(N_DEPTH, 3, LEV_DEV, TRACERS, TILE)
        for side in range(3):
            where = (region + side - 1) % N_REGION
            current = lax.dynamic_index_in_dim(total, where, 0, keepdims=False)
            total = lax.dynamic_update_index_in_dim(total, current + partial_value[:, side], where, 0)
        return total, None

    total, _ = lax.scan(visit, jnp.zeros(blocks.shape, jnp.float32), jnp.arange(N_REGION, dtype=jnp.int32))
    return total


def vertical_terms(blocks, tiles, rows, peers, targets):
    rounded = blocks.astype(jnp.bfloat16)
    tile_all = tiles.reshape(N_DEPTH, VERT_SLOTS, N_REGION, TILE, TILE)
    row_all = rows.reshape(N_DEPTH, VERT_SLOTS, N_REGION)
    peer_all = peers.reshape(N_DEPTH, VERT_SLOTS, N_REGION)
    target_all = targets.reshape(N_DEPTH, VERT_SLOTS, N_REGION)
    column_ids = jnp.arange(N_DEPTH * LEV_DEV, dtype=jnp.int32)

    def visit(carry, region):
        tile_here = lax.dynamic_index_in_dim(tile_all, region, 2, keepdims=False)
        row_here = lax.dynamic_index_in_dim(row_all, region, 2, keepdims=False)
        peer_here = lax.dynamic_index_in_dim(peer_all, region, 2, keepdims=False)
        target_here = lax.dynamic_index_in_dim(target_all, region, 2, keepdims=False)
        rounded_here = lax.dynamic_index_in_dim(rounded, region, 0, keepdims=False)
        product = slot_products(rounded_here, tile_here, row_here)
        target = peer_here * LEV_DEV + target_here
        placer = (target[:, :, None] == column_ids[None, None, :]).astype(jnp.float32)
        partial_value = jnp.einsum("dkj,dkte->djte", placer, product, precision=lax.Precision.HIGHEST)
        partial_value = lax.optimization_barrier(partial_value.astype(jnp.bfloat16)).astype(jnp.float32)
        summed = jnp.sum(partial_value, axis=0).reshape(N_DEPTH, LEV_DEV, TRACERS, TILE)
        return carry, summed

    _, terms = lax.scan(visit, jnp.zeros((), jnp.float32), jnp.arange(N_REGION, dtype=jnp.int32))
    return terms


def reference(adjoint_seed, column_lengths, lateral_tiles, lateral_rows, lateral_sides, lateral_targets, lateral_counts, vertical_tiles, vertical_rows, vertical_peers, vertical_targets):
    levels = jnp.arange(LEVELS, dtype=jnp.int32).reshape(N_DEPTH, LEV_DEV)
    lengths = column_lengths.reshape(N_REGION, TILE)
    wet = (levels[None, :, :, None, None] < lengths[:, None, None, None, :]).astype(jnp.float32)
    blocks = wet * to_blocks(adjoint_seed)

    def advance(step_index, blocks):
        blocks = wet * (blocks + vertical_terms(blocks, vertical_tiles, vertical_rows, vertical_peers, vertical_targets))
        blocks = wet * (blocks + lateral_terms(blocks, lateral_tiles, lateral_rows, lateral_sides, lateral_targets, lateral_counts))
        return blocks

    blocks = lax.fori_loop(0, STEPS, advance, blocks)
    return from_blocks(blocks)
```

```python
import functools

import jax
import jax.numpy as jnp
from jax import lax
from jax.experimental import pallas as pl
from jax.experimental.pallas import tpu as pltpu
from jax.sharding import PartitionSpec as P

STEPS = 12
GROUPS = 8
PAIR = 2
BF = jnp.bfloat16
F32 = jnp.float32


def passed_along(value, axis, by):
    devices = lax.axis_size(axis)
    return lax.ppermute(value, axis, [(i, (i + by) % devices) for i in range(devices)])


def dot(a, b):
    return jnp.dot(a, b, preferred_element_type=F32)


def placed(rows, pick_left, pick_right, tiles, place, width):
    left = dot(pick_left, rows).astype(BF)
    right = dot(pick_right, rows).astype(BF)
    slots = tiles.shape[0]
    span = 4 * width
    parts = []
    for at in range(0, slots, 4):
        part = slice(at * width, at * width + span)
        lhs = jnp.concatenate([left[part], right[part]], axis=1)
        upper = jnp.concatenate([tiles[at], tiles[at + 2]], axis=1)
        lower = jnp.concatenate([tiles[at + 1], tiles[at + 3]], axis=1)
        out = dot(lhs, jnp.concatenate([upper, lower], axis=0))
        parts.append(out[: 2 * width, :128])
        parts.append(out[2 * width :, 128:])
    product = jnp.concatenate(parts, axis=0)
    high = product.astype(BF)
    low = (product - high.astype(F32)).astype(BF)
    return dot(place, high) + dot(place, low)


def vertical_kernel(base, from_left, from_right, wet, pick_left, pick_right, place, tiles, adjoint, partial):
    value = base[...] + from_left[...].astype(F32) + from_right[...].astype(F32)
    value = wet[...] * value
    adjoint[...] = value
    partial[...] = placed(value.astype(BF), pick_left[...], pick_right[...], tiles, place[...], 16).astype(BF)


def first_kernel(seed, wet, pick_left, pick_right, place, tiles, adjoint, partial):
    value = wet[...] * seed[...]
    adjoint[...] = value
    partial[...] = placed(value.astype(BF), pick_left[...], pick_right[...], tiles, place[...], 16).astype(BF)


def lateral_kernel(adjoint, returned, wet, pick_left, pick_right, place, tiles, base, to_left, to_right):
    value = adjoint[...]
    for peer in range(GROUPS):
        value = value + returned[128 * peer : 128 * (peer + 1)].astype(F32)
    value = wet[...] * value
    partial = placed(value.astype(BF), pick_left[...], pick_right[...], tiles, place[...], 16).astype(BF)
    to_left[...] = partial[:128]
    to_right[...] = partial[256:]
    base[...] = value + partial[128:256].astype(F32)


def call(body, outs, *args):
    specs = [pl.BlockSpec(memory_space=pltpu.VMEM) for _ in args]
    return pl.pallas_call(
        body,
        out_shape=[jax.ShapeDtypeStruct(shape, kind) for shape, kind in outs],
        in_specs=specs,
        out_specs=[pl.BlockSpec(memory_space=pltpu.VMEM) for _ in outs],
        compiler_params=pltpu.CompilerParams(vmem_limit_bytes=24 * 1024 * 1024),
    )(*args)


def split_rows(field):
    levels, tracers, cells = field.shape
    shaped = field.reshape(levels, GROUPS, tracers // GROUPS, cells)
    return shaped.transpose(1, 0, 2, 3).reshape(levels * tracers, cells)


def join_rows(rows, levels, tracers):
    shaped = rows.reshape(GROUPS, levels, tracers // GROUPS, rows.shape[1])
    return shaped.transpose(1, 0, 2, 3).reshape(levels, tracers, rows.shape[1])


def level_pickers(slot_rows):
    slots = slot_rows.shape[0]
    row = jnp.arange(slots * 16, dtype=jnp.int32)
    wanted = (row % 16 // PAIR) * 16 + jnp.repeat(slot_rows, 16) * PAIR + row % PAIR
    hit = wanted[:, None] == jnp.arange(128, dtype=jnp.int32)[None, :]
    even = (row // 16 % 2 == 0)[:, None]
    return (hit & even).astype(BF), (hit & ~even).astype(BF)


def level_placer(slot_blocks, slot_levels, in_use, blocks):
    slots = slot_blocks.shape[0]
    row = jnp.arange(slots * 16, dtype=jnp.int32)
    wanted = (
        jnp.repeat(slot_blocks, 16) * 128
        + (row % 16 // PAIR) * 16
        + jnp.repeat(slot_levels, 16) * PAIR
        + row % PAIR
    )
    wanted = jnp.where(jnp.repeat(in_use, 16), wanted, -1)
    return (jnp.arange(blocks * 128, dtype=jnp.int32)[:, None] == wanted[None, :]).astype(BF)


def local(
    adjoint_seed,
    column_lengths,
    lateral_tiles,
    lateral_rows,
    lateral_sides,
    lateral_targets,
    lateral_counts,
    vertical_tiles,
    vertical_rows,
    vertical_peers,
    vertical_targets,
):
    levels_here, tracers, cells = adjoint_seed.shape
    row = jnp.arange(levels_here * tracers, dtype=jnp.int32)
    level_of_row = lax.axis_index("depth") * levels_here + row % 16 // PAIR
    wet = (level_of_row[:, None] < column_lengths[None, :]).astype(F32)

    lateral_slots = lateral_tiles.shape[0]
    in_use = jnp.arange(lateral_slots, dtype=jnp.int32) < lateral_counts[0, 0]
    lateral = (
        *level_pickers(lateral_rows[:, 0]),
        level_placer(lateral_sides[:, 0], lateral_targets[:, 0], in_use, 3),
        lateral_tiles,
    )
    vertical = (
        *level_pickers(vertical_rows[:, 0]),
        level_placer(
            vertical_peers[:, 0],
            vertical_targets[:, 0],
            jnp.ones(vertical_tiles.shape[0], jnp.bool_),
            GROUPS,
        ),
        vertical_tiles,
    )
    shape = (levels_here * tracers, cells)
    state_and_partial = [(shape, F32), ((GROUPS * shape[0], cells), BF)]
    adjoint, partial = call(first_kernel, state_and_partial, split_rows(adjoint_seed), wet, *vertical)
    for step in range(STEPS):
        returned = lax.all_to_all(partial, "depth", split_axis=0, concat_axis=0, tiled=True)
        base, to_left, to_right = call(
            lateral_kernel, [(shape, F32), (shape, BF), (shape, BF)], adjoint, returned, wet, *lateral
        )
        from_left = passed_along(to_right, "region", 1)
        from_right = passed_along(to_left, "region", -1)
        if step < STEPS - 1:
            adjoint, partial = call(
                vertical_kernel, state_and_partial, base, from_left, from_right, wet, *vertical
            )
        else:
            adjoint = wet * (base + from_left.astype(F32) + from_right.astype(F32))
    return join_rows(adjoint, levels_here, tracers)


def solution(mesh):
    return jax.shard_map(
        local,
        mesh=mesh,
        in_specs=(
            P("depth", None, "region"),
            P("region"),
            P("depth", "region", None),
            P("depth", "region"),
            P("depth", "region"),
            P("depth", "region"),
            P("depth", "region"),
            P("depth", "region", None),
            P("depth", "region"),
            P("depth", "region"),
            P("depth", "region"),
        ),
        out_specs=P("depth", None, "region"),
        check_vma=False,
    )
```

```python
import functools

import jax
import jax.numpy as jnp
from jax import lax
from jax.experimental import pallas as pl
from jax.experimental.pallas import tpu as pltpu
from jax.sharding import PartitionSpec as P

STEPS = 12
LEVEL_STEPS = 4
GROUPS = 8
PAIR = 2
BF = jnp.bfloat16
F32 = jnp.float32


def passed_along(value, axis, by):
    devices = lax.axis_size(axis)
    return lax.ppermute(value, axis, [(i, (i + by) % devices) for i in range(devices)])


def dot(a, b):
    return jnp.dot(a, b, preferred_element_type=F32)


def placed(rows, pick_left, pick_right, tiles, place, width):
    left = dot(pick_left, rows).astype(BF)
    right = dot(pick_right, rows).astype(BF)
    slots = tiles.shape[0]
    span = 4 * width
    parts = []
    for at in range(0, slots, 4):
        part = slice(at * width, at * width + span)
        lhs = jnp.concatenate([left[part], right[part]], axis=1)
        upper = jnp.concatenate([tiles[at], tiles[at + 2]], axis=1)
        lower = jnp.concatenate([tiles[at + 1], tiles[at + 3]], axis=1)
        out = dot(lhs, jnp.concatenate([upper, lower], axis=0))
        parts.append(out[: 2 * width, :128])
        parts.append(out[2 * width :, 128:])
    product = jnp.concatenate(parts, axis=0)
    high = product.astype(BF)
    low = (product - high.astype(F32)).astype(BF)
    return dot(place, high) + dot(place, low)


def vertical_kernel(base, from_left, from_right, wet, pick_left, pick_right, place, tiles, adjoint, partial):
    value = base[...] + from_left[...].astype(F32) + from_right[...].astype(F32)
    value = wet[...] * value
    adjoint[...] = value
    partial[...] = placed(value.astype(BF), pick_left[...], pick_right[...], tiles, place[...], 16).astype(BF)


def first_kernel(seed, wet, pick_left, pick_right, place, tiles, adjoint, partial):
    value = wet[...] * seed[...]
    adjoint[...] = value
    partial[...] = placed(value.astype(BF), pick_left[...], pick_right[...], tiles, place[...], 16).astype(BF)


def lateral_kernel(adjoint, returned, wet, pick_left, pick_right, place, tiles, base, to_left, to_right):
    value = adjoint[...]
    for peer in range(GROUPS):
        value = value + returned[128 * peer : 128 * (peer + 1)].astype(F32)
    value = wet[...] * value
    partial = placed(value.astype(BF), pick_left[...], pick_right[...], tiles, place[...], 16).astype(BF)
    to_left[...] = partial[:128]
    to_right[...] = partial[256:]
    base[...] = value + partial[128:256].astype(F32)


def placed_pairs(rows, pick_left, pick_right, tiles, first, slots, place, left, right, product):
    left[...] = dot(pick_left[...], rows).astype(BF)
    right[...] = dot(pick_right[...], rows).astype(BF)
    upper_rows = lax.broadcasted_iota(jnp.int32, (8, 128), 0) < 4
    blocks = tiles.shape[0] // GROUPS

    def of_depth(depth, carry):
        for octet in range(slots // 8):
            at = pl.ds(pl.multiple_of((depth * (slots // 8) + octet) * 16, 16), 16)
            lhs = jnp.concatenate([left[at], right[at]], axis=1)
            kept = []
            for quad in range(2):
                tile = depth * blocks + first + octet * 8 + quad * 4
                upper = jnp.concatenate([tiles[tile], tiles[tile + 2]], axis=1)
                lower = jnp.concatenate([tiles[tile + 1], tiles[tile + 3]], axis=1)
                out = dot(lhs, jnp.concatenate([upper, lower], axis=0))[8 * quad : 8 * quad + 8]
                kept.append(jnp.where(upper_rows, out[:, :128], out[:, 128:]))
            product[at] = jnp.concatenate(kept, axis=0)
        return carry

    lax.fori_loop(0, GROUPS, of_depth, 0)
    high = product[...].astype(BF)
    low = (product[...] - high.astype(F32)).astype(BF)
    return dot(place[...], high) + dot(place[...], low)


def tracer_step(
    value,
    wet,
    v_left,
    v_right,
    v_place,
    l_left,
    l_right,
    l_place,
    tiles,
    base,
    to_left,
    to_right,
    left,
    right,
    product,
):
    lateral_slots, vertical_slots = l_place.shape[1] // (GROUPS * PAIR), v_place.shape[1] // (GROUPS * PAIR)
    value = wet[...] * value
    part = slice(0, v_place.shape[1])
    value = value + placed_pairs(
        value.astype(BF),
        v_left,
        v_right,
        tiles,
        lateral_slots,
        vertical_slots,
        v_place,
        left.at[part],
        right.at[part],
        product.at[part],
    )
    value = wet[...] * value
    partial = placed_pairs(
        value.astype(BF), l_left, l_right, tiles, 0, lateral_slots, l_place, left, right, product
    )
    to_left[...] = partial[:128].astype(BF)
    to_right[...] = partial[256:].astype(BF)
    base[...] = value + partial[128:256]


def tracer_first_kernel(base, *refs):
    tracer_step(base[...], *refs)


def tracer_kernel(base, from_left, from_right, *refs):
    tracer_step(base[...] + from_left[...].astype(F32) + from_right[...].astype(F32), *refs)


def call(body, outs, *args, scratch=()):
    specs = [pl.BlockSpec(memory_space=pltpu.VMEM) for _ in args]
    return pl.pallas_call(
        body,
        out_shape=[jax.ShapeDtypeStruct(shape, kind) for shape, kind in outs],
        in_specs=specs,
        out_specs=[pl.BlockSpec(memory_space=pltpu.VMEM) for _ in outs],
        scratch_shapes=scratch,
        compiler_params=pltpu.CompilerParams(vmem_limit_bytes=24 * 1024 * 1024),
    )(*args)


def split_rows(field):
    levels, tracers, cells = field.shape
    shaped = field.reshape(levels, GROUPS, tracers // GROUPS, cells)
    return shaped.transpose(1, 0, 2, 3).reshape(levels * tracers, cells)


def join_rows(rows, levels, tracers):
    shaped = rows.reshape(GROUPS, levels, tracers // GROUPS, rows.shape[1])
    return shaped.transpose(1, 0, 2, 3).reshape(levels, tracers, rows.shape[1])


def level_pickers(slot_rows):
    slots = slot_rows.shape[0]
    row = jnp.arange(slots * 16, dtype=jnp.int32)
    wanted = (row % 16 // PAIR) * 16 + jnp.repeat(slot_rows, 16) * PAIR + row % PAIR
    hit = wanted[:, None] == jnp.arange(128, dtype=jnp.int32)[None, :]
    even = (row // 16 % 2 == 0)[:, None]
    return (hit & even).astype(BF), (hit & ~even).astype(BF)


def level_placer(slot_blocks, slot_levels, in_use, blocks):
    slots = slot_blocks.shape[0]
    row = jnp.arange(slots * 16, dtype=jnp.int32)
    wanted = (
        jnp.repeat(slot_blocks, 16) * 128
        + (row % 16 // PAIR) * 16
        + jnp.repeat(slot_levels, 16) * PAIR
        + row % PAIR
    )
    wanted = jnp.where(jnp.repeat(in_use, 16), wanted, -1)
    return (jnp.arange(blocks * 128, dtype=jnp.int32)[:, None] == wanted[None, :]).astype(BF)


def tracer_pickers(slot_rows):
    depths, slots = slot_rows.shape
    row = jnp.arange(depths * slots * PAIR, dtype=jnp.int32)
    wanted = (row // (slots * PAIR) * 8 + jnp.repeat(slot_rows.reshape(-1), PAIR)) * PAIR + row % PAIR
    hit = wanted[:, None] == jnp.arange(128, dtype=jnp.int32)[None, :]
    even = (row // PAIR % 2 == 0)[:, None]
    return (hit & even).astype(BF), (hit & ~even).astype(BF)


def tracer_placer(blocks, count):
    pair = jnp.arange(blocks.shape[0] * PAIR, dtype=jnp.int32) % PAIR
    wanted = jnp.repeat(blocks, PAIR) * PAIR + pair
    return (jnp.arange(count * PAIR, dtype=jnp.int32)[:, None] == wanted[None, :]).astype(BF)


def gather_tiles(lateral_tiles, lateral_rows, lateral_blocks, vertical_tiles, vertical_rows, vertical_blocks):
    lists = [lateral_rows, lateral_blocks, vertical_rows, vertical_blocks]
    lists = jnp.stack([jnp.pad(entry, (0, 128 - entry.shape[0])) for entry in lists]).astype(BF)
    lists = jnp.pad(lists, ((0, 128 - lists.shape[0]), (0, 0)))
    own = jnp.concatenate([lateral_tiles, vertical_tiles, lists[None]], axis=0)
    return lax.all_gather(own, "depth", axis=0, tiled=True)


def local(
    adjoint_seed,
    column_lengths,
    lateral_tiles,
    lateral_rows,
    lateral_sides,
    lateral_targets,
    lateral_counts,
    vertical_tiles,
    vertical_rows,
    vertical_peers,
    vertical_targets,
):
    levels_here, tracers, cells = adjoint_seed.shape
    gathered = gather_tiles(
        lateral_tiles,
        lateral_rows[:, 0],
        jnp.where(
            jnp.arange(lateral_tiles.shape[0], dtype=jnp.int32) < lateral_counts[0, 0],
            lateral_sides[:, 0] * levels_here + lateral_targets[:, 0],
            -1,
        ),
        vertical_tiles,
        vertical_rows[:, 0],
        vertical_peers[:, 0] * levels_here + vertical_targets[:, 0],
    )
    row = jnp.arange(levels_here * tracers, dtype=jnp.int32)
    level_of_row = lax.axis_index("depth") * levels_here + row % 16 // PAIR
    wet = (level_of_row[:, None] < column_lengths[None, :]).astype(F32)

    lateral_slots = lateral_tiles.shape[0]
    in_use = jnp.arange(lateral_slots, dtype=jnp.int32) < lateral_counts[0, 0]
    lateral = (
        *level_pickers(lateral_rows[:, 0]),
        level_placer(lateral_sides[:, 0], lateral_targets[:, 0], in_use, 3),
        lateral_tiles,
    )
    vertical = (
        *level_pickers(vertical_rows[:, 0]),
        level_placer(
            vertical_peers[:, 0],
            vertical_targets[:, 0],
            jnp.ones(vertical_tiles.shape[0], jnp.bool_),
            GROUPS,
        ),
        vertical_tiles,
    )
    shape = (levels_here * tracers, cells)
    state_and_partial = [(shape, F32), ((GROUPS * shape[0], cells), BF)]
    adjoint, partial = call(first_kernel, state_and_partial, split_rows(adjoint_seed), wet, *vertical)
    exchanged = [(shape, F32), (shape, BF), (shape, BF)]
    for step in range(LEVEL_STEPS):
        returned = lax.all_to_all(partial, "depth", split_axis=0, concat_axis=0, tiled=True)
        base, to_left, to_right = call(lateral_kernel, exchanged, adjoint, returned, wet, *lateral)
        from_left = passed_along(to_right, "region", 1)
        from_right = passed_along(to_left, "region", -1)
        if step < LEVEL_STEPS - 1:
            adjoint, partial = call(
                vertical_kernel, state_and_partial, base, from_left, from_right, wet, *vertical
            )

    vertical_slots = vertical_tiles.shape[0]
    per_depth = lateral_slots + vertical_slots + 1
    lists = gathered.reshape(GROUPS, per_depth, 128, 128)[:, -1, :4].astype(jnp.int32)
    level = jnp.arange(shape[0], dtype=jnp.int32) // PAIR
    lateral_blocks = lists[:, 1, :lateral_slots]
    lateral_level = jnp.arange(GROUPS, dtype=jnp.int32)[:, None] * levels_here + lateral_blocks % levels_here
    lateral_blocks = jnp.where(
        lateral_blocks < 0, -1, lateral_blocks // levels_here * (GROUPS * levels_here) + lateral_level
    )
    constants = (
        (level[:, None] < column_lengths[None, :]).astype(F32),
        *tracer_pickers(lists[:, 2, :vertical_slots]),
        tracer_placer(lists[:, 3, :vertical_slots].reshape(-1), GROUPS * levels_here),
        *tracer_pickers(lists[:, 0, :lateral_slots]),
        tracer_placer(lateral_blocks.reshape(-1), 3 * GROUPS * levels_here),
        gathered,
    )
    rows = GROUPS * lateral_slots * PAIR
    scratch = (pltpu.VMEM((rows, 128), BF), pltpu.VMEM((rows, 128), BF), pltpu.VMEM((rows, 128), F32))
    value = base + from_left.astype(F32) + from_right.astype(F32)
    value = lax.all_to_all(value, "depth", split_axis=0, concat_axis=0, tiled=True)
    for step in range(LEVEL_STEPS, STEPS):
        if step == LEVEL_STEPS:
            received, body = (value,), tracer_first_kernel
        else:
            received, body = (base, from_left, from_right), tracer_kernel
        base, to_left, to_right = call(body, exchanged, *received, *constants, scratch=scratch)
        from_left = passed_along(to_right, "region", 1)
        from_right = passed_along(to_left, "region", -1)
    value = base + from_left.astype(F32) + from_right.astype(F32)
    adjoint = wet * lax.all_to_all(value, "depth", split_axis=0, concat_axis=0, tiled=True)
    return join_rows(adjoint, levels_here, tracers)


def solution(mesh):
    return jax.shard_map(
        local,
        mesh=mesh,
        in_specs=(
            P("depth", None, "region"),
            P("region"),
            P("depth", "region", None),
            P("depth", "region"),
            P("depth", "region"),
            P("depth", "region"),
            P("depth", "region"),
            P("depth", "region", None),
            P("depth", "region"),
            P("depth", "region"),
            P("depth", "region"),
        ),
        out_specs=P("depth", None, "region"),
        check_vma=False,
    )
```

```python
import jax
import jax.numpy as jnp
from jax import lax
from jax.experimental import pallas as pl
from jax.experimental.pallas import tpu as pltpu
from jax.sharding import PartitionSpec as P

STEPS = 12
LEVEL_STEPS = 4
GROUPS = 8
PAIR = 2
LEVELS = 8
TRACERS = GROUPS * PAIR
CELLS = 128
STATE = 128
LISTS = 16
BF = jnp.bfloat16
F32 = jnp.float32
I32 = jnp.int32


def dot(a, b):
    return jnp.dot(a, b, preferred_element_type=F32)


def dot_last(a, b):
    return lax.dot_general(a, b, (((1,), (1,)), ((), ())), preferred_element_type=F32)


def iota(shape, dim):
    return lax.broadcasted_iota(I32, shape, dim)


def spread(codes, slots, rows):
    owner = (iota((slots * rows, CELLS), 0) // rows == iota((slots * rows, CELLS), 1)).astype(BF)
    return dot_last(owner, codes).astype(I32), dot_last(codes, owner).astype(I32)


def write_picks(wanted, rows, left, right, part=slice(None)):
    count = wanted.shape[0]
    hit = jnp.where(wanted == iota((count, STATE), 1), 1.0, 0.0)
    even = iota((count, STATE), 0) // rows % 2 == 0
    left[part] = jnp.where(even, hit, 0.0).astype(BF)
    right[part] = jnp.where(even, 0.0, hit).astype(BF)


def write_place(wanted, place, part=slice(None)):
    shape = (place.shape[0], wanted.shape[1])
    place[:, part] = jnp.where(wanted == iota(shape, 0), 1.0, 0.0).astype(BF)


def level_matrices(codes, row_of, block_of, slots, left, right, place):
    columns, rows = spread(codes, slots, TRACERS)
    tracer = iota((slots * TRACERS, 1), 0) % TRACERS
    wanted = tracer // PAIR * TRACERS + columns[:, row_of : row_of + 1] * PAIR + tracer % PAIR
    write_picks(wanted, TRACERS, left, right)
    tracer = iota((1, slots * TRACERS), 1) % TRACERS
    block = rows[block_of : block_of + 1]
    wanted = block // LEVELS * STATE + tracer // PAIR * TRACERS + block % LEVELS * PAIR + tracer % PAIR
    write_place(jnp.where(block < 0, -1, wanted), place)


def level_products(rows, left, right, place, tiles):
    rows = rows.astype(BF)
    x_left = dot(left[...], rows).astype(BF)
    x_right = dot(right[...], rows).astype(BF)
    parts = []
    for at in range(0, tiles.shape[0], 4):
        part = slice(at * TRACERS, (at + 4) * TRACERS)
        lhs = jnp.concatenate([x_left[part], x_right[part]], axis=1)
        upper = jnp.concatenate([tiles[at], tiles[at + 2]], axis=1)
        lower = jnp.concatenate([tiles[at + 1], tiles[at + 3]], axis=1)
        out = dot(lhs, jnp.concatenate([upper, lower], axis=0))
        parts += [out[: 2 * TRACERS, :CELLS], out[2 * TRACERS :, CELLS:]]
    return placed(place, jnp.concatenate(parts, axis=0))


def placed(place, product):
    high = product.astype(BF)
    low = (product - high.astype(F32)).astype(BF)
    return dot(place[...], high) + dot(place[...], low)


def open_kernel(
    seed, lengths, l_rows, l_sides, l_targets, l_count, v_rows, v_peers, v_targets, tiles,
    adjoint, partial, wet, left, right, place, codes,
):
    l_slots, v_slots = l_rows.shape[1], v_rows.shape[1]
    codes[...] = jnp.zeros(codes.shape, F32)
    odd = lax.axis_index("region") % 2
    side = jnp.where(odd == 1, 2 - l_sides[...], l_sides[...])
    used = iota((1, l_slots), 1) < l_count[...]
    codes[0:1, 0:l_slots] = l_rows[...].astype(F32)
    codes[1:2, 0:l_slots] = jnp.where(used, side * LEVELS + l_targets[...], -1).astype(F32)
    codes[2:3, 0:v_slots] = v_rows[...].astype(F32)
    codes[3:4, 0:v_slots] = (v_peers[...] * LEVELS + v_targets[...]).astype(F32)
    level = lax.axis_index("depth") * LEVELS + iota((STATE, CELLS), 0) % TRACERS // PAIR
    wet[...] = jnp.where(level < lengths[...], 1.0, 0.0)
    level_matrices(codes[...].astype(BF)[:8], 2, 3, v_slots, left, right, place)
    for group in range(GROUPS):
        for at in range(LEVELS):
            row = group * TRACERS + at * PAIR
            adjoint[row : row + PAIR] = seed[at, group * PAIR : group * PAIR + PAIR]
    value = wet[...] * adjoint[...]
    adjoint[...] = value
    sums = level_products(value, left, right, place, tiles).astype(BF)
    for peer in range(GROUPS):
        at = peer * (STATE + LISTS)
        partial[at : at + STATE] = sums[peer * STATE : (peer + 1) * STATE]
        partial[at + STATE : at + STATE + LISTS] = codes[...].astype(BF)


def lateral_lists_kernel(codes, left, right, place):
    level_matrices(codes[...].astype(BF)[:8], 0, 1, left.shape[0] // TRACERS, left, right, place)


def vertical_kernel(base, first, second, wet, left, right, place, tiles, adjoint, partial):
    value = wet[...] * (base[...] + first[...].astype(F32) + second[...].astype(F32))
    adjoint[...] = value
    partial[...] = level_products(value, left, right, place, tiles).astype(BF)


def lateral_kernel(adjoint, returned, wet, left, right, place, tiles, base, to_first, to_second):
    value = adjoint[...]
    stride = returned.shape[0] // GROUPS
    for peer in range(GROUPS):
        value = value + returned[stride * peer : stride * peer + STATE].astype(F32)
    value = wet[...] * value
    partial = level_products(value, left, right, place, tiles).astype(BF)
    to_first[...] = partial[:STATE]
    to_second[...] = partial[2 * STATE :]
    base[...] = value + partial[STATE : 2 * STATE].astype(F32)


def tracer_lists_kernel(returned, lengths, wet, v_left, v_right, v_place, l_left, l_right, l_place):
    level = iota((STATE, CELLS), 0) // PAIR
    wet[...] = jnp.where(level < lengths[...], 1.0, 0.0)
    l_rows, v_rows = l_left.shape[0] // GROUPS, v_left.shape[0] // GROUPS
    stride = STATE + LISTS
    for depth in range(GROUPS):
        codes = returned[depth * stride + STATE : (depth + 1) * stride][:8]
        for rows, row_of, left, right in ((l_rows, 0, l_left, l_right), (v_rows, 2, v_left, v_right)):
            columns, lines = spread(codes, rows // PAIR, PAIR)
            part = slice(depth * rows, (depth + 1) * rows)
            wanted = (depth * LEVELS + columns[:, row_of : row_of + 1]) * PAIR + iota((rows, 1), 0) % PAIR
            write_picks(wanted, PAIR, left, right, part)
            block = lines[row_of + 1 : row_of + 2]
            pair = iota((1, rows), 1) % PAIR
            if row_of == 0:
                wanted = block // LEVELS * STATE + (depth * LEVELS + block % LEVELS) * PAIR + pair
                wanted = jnp.where(block < 0, -1, wanted)
                write_place(wanted, l_place.at[depth])
            else:
                write_place(block * PAIR + pair, v_place.at[depth])


def tracer_products(rows, left, right, place, tiles, first, slots):
    rows = rows.astype(BF)
    x_left = dot(left[...], rows).astype(BF)
    x_right = dot(right[...], rows).astype(BF)
    upper_rows = iota((8, CELLS), 0) < 2 * PAIR
    blocks = tiles.shape[0] // GROUPS
    total = None
    for depth in range(GROUPS):
        parts = []
        for octet in range(slots // 8):
            at = (depth * slots + octet * 8) * PAIR
            part = slice(at, at + 8 * PAIR)
            lhs = jnp.concatenate([x_left[part], x_right[part]], axis=1)
            for quad in range(2):
                tile = depth * blocks + first + octet * 8 + quad * 4
                upper = jnp.concatenate([tiles[tile], tiles[tile + 2]], axis=1)
                lower = jnp.concatenate([tiles[tile + 1], tiles[tile + 3]], axis=1)
                out = dot(lhs, jnp.concatenate([upper, lower], axis=0))[8 * quad : 8 * quad + 8]
                parts.append(jnp.where(upper_rows, out[:, :CELLS], out[:, CELLS:]))
        sums = placed(place.at[depth], jnp.concatenate(parts, axis=0))
        total = sums if total is None else total + sums
    return total


def tracer_step(value, wet, v_left, v_right, v_place, l_left, l_right, l_place, tiles, base, to_first, to_second):
    l_slots, v_slots = l_left.shape[0] // (GROUPS * PAIR), v_left.shape[0] // (GROUPS * PAIR)
    value = wet[...] * value
    value = wet[...] * (value + tracer_products(value, v_left, v_right, v_place, tiles, l_slots, v_slots))
    partial = tracer_products(value, l_left, l_right, l_place, tiles, 0, l_slots)
    to_first[...] = partial[:STATE].astype(BF)
    to_second[...] = partial[2 * STATE :].astype(BF)
    base[...] = value + partial[STATE : 2 * STATE]


def tracer_first_kernel(value, *refs):
    tracer_step(value[...], *refs)


def tracer_kernel(base, first, second, *refs):
    tracer_step(base[...] + first[...].astype(F32) + second[...].astype(F32), *refs)


def sum_kernel(base, first, second, total):
    total[...] = base[...] + first[...].astype(F32) + second[...].astype(F32)


def close_kernel(value, wet, out):
    rows = wet[...] * value[...]
    for group in range(GROUPS):
        for at in range(LEVELS):
            row = group * TRACERS + at * PAIR
            out[at, group * PAIR : group * PAIR + PAIR] = rows[row : row + PAIR]


def call(body, outs, *args, scratch=()):
    return pl.pallas_call(
        body,
        out_shape=[jax.ShapeDtypeStruct(shape, kind) for shape, kind in outs],
        in_specs=[pl.BlockSpec(memory_space=pltpu.VMEM) for _ in args],
        out_specs=[pl.BlockSpec(memory_space=pltpu.VMEM) for _ in outs],
        scratch_shapes=scratch,
        compiler_params=pltpu.CompilerParams(vmem_limit_bytes=24 * 1024 * 1024),
    )(*args)


def swapped(to_first, to_second):
    regions = lax.axis_size("region")
    first = [(i, (i + 1) % regions if i % 2 else (i - 1) % regions) for i in range(regions)]
    second = [(i, i ^ 1) for i in range(regions)]
    from_first = lax.ppermute(to_first, "region", first)
    from_second = lax.ppermute(to_second, "region", second)
    return from_first, from_second


def to_depth(value):
    return lax.all_to_all(value, "depth", split_axis=0, concat_axis=0, tiled=True)


def local(
    adjoint_seed,
    column_lengths,
    lateral_tiles,
    lateral_rows,
    lateral_sides,
    lateral_targets,
    lateral_counts,
    vertical_tiles,
    vertical_rows,
    vertical_peers,
    vertical_targets,
):
    gathered = lax.all_gather(
        jnp.concatenate([lateral_tiles, vertical_tiles], axis=0), "depth", axis=0, tiled=True
    )
    l_slots, v_slots = lateral_tiles.shape[0], vertical_tiles.shape[0]
    lengths = column_lengths.reshape(1, CELLS)
    state = ((STATE, CELLS), F32)
    sent = ((STATE, CELLS), BF)

    def matrices(slots, blocks):
        return [((slots * TRACERS, STATE), BF)] * 2 + [((blocks * STATE, slots * TRACERS), BF)]

    adjoint, partial, wet, *vertical, codes = call(
        open_kernel,
        [state, ((GROUPS * (STATE + LISTS), CELLS), BF), state]
        + matrices(v_slots, GROUPS)
        + [((LISTS, CELLS), F32)],
        adjoint_seed,
        lengths,
        lateral_rows.reshape(1, l_slots),
        lateral_sides.reshape(1, l_slots),
        lateral_targets.reshape(1, l_slots),
        lateral_counts,
        vertical_rows.reshape(1, v_slots),
        vertical_peers.reshape(1, v_slots),
        vertical_targets.reshape(1, v_slots),
        vertical_tiles,
    )
    lateral = call(lateral_lists_kernel, matrices(l_slots, 3), codes)
    returned = first_returned = to_depth(partial)
    for step in range(LEVEL_STEPS):
        base, to_first, to_second = call(
            lateral_kernel, [state, sent, sent], adjoint, returned, wet, *lateral, lateral_tiles
        )
        received = swapped(to_first, to_second)
        if step < LEVEL_STEPS - 1:
            adjoint, partial = call(
                vertical_kernel,
                [state, ((GROUPS * STATE, CELLS), BF)],
                base,
                *received,
                wet,
                *vertical,
                vertical_tiles,
            )
            returned = to_depth(partial)

    def tracer_matrices(slots, blocks):
        rows = slots * PAIR
        return [((GROUPS * rows, STATE), BF)] * 2 + [((GROUPS, blocks * STATE, rows), BF)]

    constants = call(
        tracer_lists_kernel,
        [state] + tracer_matrices(v_slots, 1) + tracer_matrices(l_slots, 3),
        first_returned,
        lengths,
    )
    (value,) = call(sum_kernel, [state], base, *received)
    value, gathered = lax.optimization_barrier((value, gathered))
    value = to_depth(value)
    for step in range(LEVEL_STEPS, STEPS):
        if step == LEVEL_STEPS:
            arrived, body = (value,), tracer_first_kernel
        else:
            arrived, body = (base, *received), tracer_kernel
        base, to_first, to_second = call(body, [state, sent, sent], *arrived, *constants, gathered)
        received = swapped(to_first, to_second)
    (value,) = call(sum_kernel, [state], base, *received)
    (adjoint,) = call(close_kernel, [((LEVELS, TRACERS, CELLS), F32)], to_depth(value), wet)
    return adjoint


def solution(mesh):
    return jax.shard_map(
        local,
        mesh=mesh,
        in_specs=(
            P("depth", None, "region"),
            P("region"),
            P("depth", "region", None),
            P("depth", "region"),
            P("depth", "region"),
            P("depth", "region"),
            P("depth", "region"),
            P("depth", "region", None),
            P("depth", "region"),
            P("depth", "region"),
            P("depth", "region"),
        ),
        out_specs=P("depth", None, "region"),
        check_vma=False,
    )
```

```python
import jax
import jax.numpy as jnp
from jax import lax
from jax.experimental import pallas as pl
from jax.experimental.pallas import tpu as pltpu
from jax.sharding import PartitionSpec as P

STEPS = 12
LEVEL_STEPS = 4
GROUPS = 8
PAIR = 2
LEVELS = 8
TRACERS = GROUPS * PAIR
CELLS = 128
STATE = 128
LISTS = 16
BF = jnp.bfloat16
F32 = jnp.float32
I32 = jnp.int32


def dot(a, b):
    return jnp.dot(a, b, preferred_element_type=F32)


def dot_last(a, b):
    return lax.dot_general(a, b, (((1,), (1,)), ((), ())), preferred_element_type=F32)


def iota(shape, dim):
    return lax.broadcasted_iota(I32, shape, dim)


def spread(codes, slots, rows):
    owner = (iota((slots * rows, CELLS), 0) // rows == iota((slots * rows, CELLS), 1)).astype(BF)
    return dot_last(owner, codes).astype(I32), dot_last(codes, owner).astype(I32)


def write_picks(wanted, rows, left, right, part=slice(None)):
    count = wanted.shape[0]
    hit = jnp.where(wanted == iota((count, STATE), 1), 1.0, 0.0)
    even = iota((count, STATE), 0) // rows % 2 == 0
    left[part] = jnp.where(even, hit, 0.0).astype(BF)
    right[part] = jnp.where(even, 0.0, hit).astype(BF)


def write_place(wanted, place, part=slice(None)):
    shape = (place.shape[0], wanted.shape[1])
    place[:, part] = jnp.where(wanted == iota(shape, 0), 1.0, 0.0).astype(BF)


def level_matrices(codes, row_of, block_of, slots, left, right, place):
    columns, rows = spread(codes, slots, TRACERS)
    tracer = iota((slots * TRACERS, 1), 0) % TRACERS
    wanted = tracer // PAIR * TRACERS + columns[:, row_of : row_of + 1] * PAIR + tracer % PAIR
    write_picks(wanted, TRACERS, left, right)
    tracer = iota((1, slots * TRACERS), 1) % TRACERS
    block = rows[block_of : block_of + 1]
    wanted = block // LEVELS * STATE + tracer // PAIR * TRACERS + block % LEVELS * PAIR + tracer % PAIR
    write_place(jnp.where(block < 0, -1, wanted), place)


def level_products(rows, left, right, place, tiles):
    rows = rows.astype(BF)
    x_left = dot(left[...], rows).astype(BF)
    x_right = dot(right[...], rows).astype(BF)
    parts = []
    for at in range(0, tiles.shape[0], 4):
        part = slice(at * TRACERS, (at + 4) * TRACERS)
        lhs = jnp.concatenate([x_left[part], x_right[part]], axis=1)
        upper = jnp.concatenate([tiles[at], tiles[at + 2]], axis=1)
        lower = jnp.concatenate([tiles[at + 1], tiles[at + 3]], axis=1)
        out = dot(lhs, jnp.concatenate([upper, lower], axis=0))
        parts += [out[: 2 * TRACERS, :CELLS], out[2 * TRACERS :, CELLS:]]
    return placed(place, jnp.concatenate(parts, axis=0))


def placed(place, product):
    high = product.astype(BF)
    low = (product - high.astype(F32)).astype(BF)
    return dot(place[...], high) + dot(place[...], low)


def open_kernel(
    seed, lengths, l_rows, l_sides, l_targets, l_count, v_rows, v_peers, v_targets, tiles,
    adjoint, partial, wet, left, right, place, codes,
):
    l_slots, v_slots = l_rows.shape[1], v_rows.shape[1]
    codes[...] = jnp.zeros(codes.shape, F32)
    odd = lax.axis_index("region") % 2
    side = jnp.where(odd == 1, 2 - l_sides[...], l_sides[...])
    used = iota((1, l_slots), 1) < l_count[...]
    codes[0:1, 0:l_slots] = l_rows[...].astype(F32)
    codes[1:2, 0:l_slots] = jnp.where(used, side * LEVELS + l_targets[...], -1).astype(F32)
    codes[2:3, 0:v_slots] = v_rows[...].astype(F32)
    codes[3:4, 0:v_slots] = (v_peers[...] * LEVELS + v_targets[...]).astype(F32)
    level = lax.axis_index("depth") * LEVELS + iota((STATE, CELLS), 0) % TRACERS // PAIR
    wet[...] = jnp.where(level < lengths[...], 1.0, 0.0)
    level_matrices(codes[...].astype(BF)[:8], 2, 3, v_slots, left, right, place)
    for group in range(GROUPS):
        for at in range(LEVELS):
            row = group * TRACERS + at * PAIR
            adjoint[row : row + PAIR] = seed[at, group * PAIR : group * PAIR + PAIR]
    value = wet[...] * adjoint[...]
    adjoint[...] = value
    sums = level_products(value, left, right, place, tiles).astype(BF)
    for peer in range(GROUPS):
        at = peer * (STATE + LISTS)
        partial[at : at + STATE] = sums[peer * STATE : (peer + 1) * STATE]
        partial[at + STATE : at + STATE + LISTS] = codes[...].astype(BF)


def lateral_lists_kernel(codes, left, right, place):
    level_matrices(codes[...].astype(BF)[:8], 0, 1, left.shape[0] // TRACERS, left, right, place)


def vertical_kernel(base, first, second, wet, left, right, place, tiles, adjoint, partial):
    value = wet[...] * (base[...] + first[...].astype(F32) + second[...].astype(F32))
    adjoint[...] = value
    partial[...] = level_products(value, left, right, place, tiles).astype(BF)


def lateral_kernel(adjoint, returned, wet, left, right, place, tiles, base, to_first, to_second):
    value = adjoint[...]
    stride = returned.shape[0] // GROUPS
    for peer in range(GROUPS):
        value = value + returned[stride * peer : stride * peer + STATE].astype(F32)
    value = wet[...] * value
    partial = level_products(value, left, right, place, tiles).astype(BF)
    to_first[...] = partial[:STATE]
    to_second[...] = partial[2 * STATE :]
    base[...] = value + partial[STATE : 2 * STATE].astype(F32)


def tracer_lists_kernel(returned, lengths, wet, v_left, v_right, v_place, l_left, l_right, l_place, lines_l, lines_v):
    level = iota((STATE, CELLS), 0) // PAIR
    wet[...] = jnp.where(level < lengths[...], 1.0, 0.0)
    l_rows, v_rows = l_left.shape[0] // GROUPS, v_left.shape[0] // GROUPS
    stride = STATE + LISTS
    for depth in range(GROUPS):
        codes = returned[depth * stride + STATE : (depth + 1) * stride][:8]
        for rows, row_of, left, right in ((l_rows, 0, l_left, l_right), (v_rows, 2, v_left, v_right)):
            columns, lines = spread(codes, rows // PAIR, PAIR)
            part = slice(depth * rows, (depth + 1) * rows)
            wanted = (depth * LEVELS + columns[:, row_of : row_of + 1]) * PAIR + iota((rows, 1), 0) % PAIR
            write_picks(wanted, PAIR, left, right, part)
            block = lines[row_of + 1 : row_of + 2]
            pair = iota((1, rows), 1) % PAIR
            if row_of == 0:
                wanted = block // LEVELS * STATE + (depth * LEVELS + block % LEVELS) * PAIR + pair
                wanted = jnp.where(block < 0, -1, wanted)
            else:
                wanted = block * PAIR + pair
            line = lines_l if row_of == 0 else lines_v
            line[:, part] = jnp.broadcast_to(wanted, (8, rows))
    write_place(lines_l[0:1], l_place)
    write_place(lines_v[0:1], v_place)


def tracer_products(rows, left, right, place, tiles, first, slots, scratch):
    x_left, x_right, product = scratch
    count = left.shape[0]
    rows = rows.astype(BF)
    x_left[:count] = dot(left[...], rows).astype(BF)
    x_right[:count] = dot(right[...], rows).astype(BF)
    upper_rows = iota((8, CELLS), 0) < 2 * PAIR
    blocks = tiles.shape[0] // GROUPS
    for depth in range(GROUPS):
        for octet in range(slots // 8):
            at = (depth * slots + octet * 8) * PAIR
            part = slice(at, at + 8 * PAIR)
            lhs = jnp.concatenate([x_left[part], x_right[part]], axis=1)
            for quad in range(2):
                tile = depth * blocks + first + octet * 8 + quad * 4
                upper = jnp.concatenate([tiles[tile], tiles[tile + 2]], axis=1)
                lower = jnp.concatenate([tiles[tile + 1], tiles[tile + 3]], axis=1)
                out = dot(lhs, jnp.concatenate([upper, lower], axis=0))[8 * quad : 8 * quad + 8]
                product[at + 8 * quad : at + 8 * quad + 8] = jnp.where(upper_rows, out[:, :CELLS], out[:, CELLS:])
    return placed(place, product[:count])


def tracer_step(value, wet, v_left, v_right, v_place, l_left, l_right, l_place, tiles, base, to_first, to_second, *scratch):
    l_slots, v_slots = l_left.shape[0] // (GROUPS * PAIR), v_left.shape[0] // (GROUPS * PAIR)
    value = wet[...] * value
    value = wet[...] * (value + tracer_products(value, v_left, v_right, v_place, tiles, l_slots, v_slots, scratch))
    partial = tracer_products(value, l_left, l_right, l_place, tiles, 0, l_slots, scratch)
    to_first[...] = partial[:STATE].astype(BF)
    to_second[...] = partial[2 * STATE :].astype(BF)
    base[...] = value + partial[STATE : 2 * STATE]


def tracer_first_kernel(value, *refs):
    tracer_step(value[...], *refs)


def tracer_kernel(base, first, second, *refs):
    tracer_step(base[...] + first[...].astype(F32) + second[...].astype(F32), *refs)


def sum_kernel(base, first, second, total):
    total[...] = base[...] + first[...].astype(F32) + second[...].astype(F32)


def close_kernel(value, wet, out):
    rows = wet[...] * value[...]
    for group in range(GROUPS):
        for at in range(LEVELS):
            row = group * TRACERS + at * PAIR
            out[at, group * PAIR : group * PAIR + PAIR] = rows[row : row + PAIR]


def call(body, outs, *args, scratch=()):
    return pl.pallas_call(
        body,
        out_shape=[jax.ShapeDtypeStruct(shape, kind) for shape, kind in outs],
        in_specs=[pl.BlockSpec(memory_space=pltpu.VMEM) for _ in args],
        out_specs=[pl.BlockSpec(memory_space=pltpu.VMEM) for _ in outs],
        scratch_shapes=scratch,
        compiler_params=pltpu.CompilerParams(vmem_limit_bytes=24 * 1024 * 1024),
    )(*args)


def swapped(to_first, to_second):
    regions = lax.axis_size("region")
    first = [(i, (i + 1) % regions if i % 2 else (i - 1) % regions) for i in range(regions)]
    second = [(i, i ^ 1) for i in range(regions)]
    from_first = lax.ppermute(to_first, "region", first)
    from_second = lax.ppermute(to_second, "region", second)
    return from_first, from_second


def to_depth(value):
    return lax.all_to_all(value, "depth", split_axis=0, concat_axis=0, tiled=True)


def local(
    adjoint_seed,
    column_lengths,
    lateral_tiles,
    lateral_rows,
    lateral_sides,
    lateral_targets,
    lateral_counts,
    vertical_tiles,
    vertical_rows,
    vertical_peers,
    vertical_targets,
):
    gathered = lax.all_gather(
        jnp.concatenate([lateral_tiles, vertical_tiles], axis=0), "depth", axis=0, tiled=True
    )
    l_slots, v_slots = lateral_tiles.shape[0], vertical_tiles.shape[0]
    lengths = column_lengths.reshape(1, CELLS)
    state = ((STATE, CELLS), F32)
    sent = ((STATE, CELLS), BF)

    def matrices(slots, blocks):
        return [((slots * TRACERS, STATE), BF)] * 2 + [((blocks * STATE, slots * TRACERS), BF)]

    adjoint, partial, wet, *vertical, codes = call(
        open_kernel,
        [state, ((GROUPS * (STATE + LISTS), CELLS), BF), state]
        + matrices(v_slots, GROUPS)
        + [((LISTS, CELLS), F32)],
        adjoint_seed,
        lengths,
        lateral_rows.reshape(1, l_slots),
        lateral_sides.reshape(1, l_slots),
        lateral_targets.reshape(1, l_slots),
        lateral_counts,
        vertical_rows.reshape(1, v_slots),
        vertical_peers.reshape(1, v_slots),
        vertical_targets.reshape(1, v_slots),
        vertical_tiles,
    )
    lateral = call(lateral_lists_kernel, matrices(l_slots, 3), codes)
    returned = first_returned = to_depth(partial)
    for step in range(LEVEL_STEPS):
        base, to_first, to_second = call(
            lateral_kernel, [state, sent, sent], adjoint, returned, wet, *lateral, lateral_tiles
        )
        received = swapped(to_first, to_second)
        if step < LEVEL_STEPS - 1:
            adjoint, partial = call(
                vertical_kernel,
                [state, ((GROUPS * STATE, CELLS), BF)],
                base,
                *received,
                wet,
                *vertical,
                vertical_tiles,
            )
            returned = to_depth(partial)

    def tracer_matrices(slots, blocks):
        rows = slots * PAIR
        return [((GROUPS * rows, STATE), BF)] * 2 + [((blocks * STATE, GROUPS * rows), BF)]

    constants = call(
        tracer_lists_kernel,
        [state] + tracer_matrices(v_slots, 1) + tracer_matrices(l_slots, 3),
        first_returned,
        lengths,
        scratch=[pltpu.VMEM((8, GROUPS * slots * PAIR), I32) for slots in (l_slots, v_slots)],
    )
    rows = GROUPS * l_slots * PAIR
    scratch = [pltpu.VMEM((rows, CELLS), kind) for kind in (BF, BF, F32)]
    (value,) = call(sum_kernel, [state], base, *received)
    value, gathered = lax.optimization_barrier((value, gathered))
    value = to_depth(value)
    for step in range(LEVEL_STEPS, STEPS):
        if step == LEVEL_STEPS:
            arrived, body = (value,), tracer_first_kernel
        else:
            arrived, body = (base, *received), tracer_kernel
        base, to_first, to_second = call(body, [state, sent, sent], *arrived, *constants, gathered, scratch=scratch)
        received = swapped(to_first, to_second)
    (value,) = call(sum_kernel, [state], base, *received)
    (adjoint,) = call(close_kernel, [((LEVELS, TRACERS, CELLS), F32)], to_depth(value), wet)
    return adjoint


def solution(mesh):
    return jax.shard_map(
        local,
        mesh=mesh,
        in_specs=(
            P("depth", None, "region"),
            P("region"),
            P("depth", "region", None),
            P("depth", "region"),
            P("depth", "region"),
            P("depth", "region"),
            P("depth", "region"),
            P("depth", "region", None),
            P("depth", "region"),
            P("depth", "region"),
            P("depth", "region"),
        ),
        out_specs=P("depth", None, "region"),
        check_vma=False,
    )
```

```python
import jax
import jax.numpy as jnp
from jax import lax
from jax.experimental import pallas as pl
from jax.experimental.pallas import tpu as pltpu
from jax.sharding import PartitionSpec as P

STEPS = 12
LEVEL_STEPS = 3
GROUPS = 8
PAIR = 2
LEVELS = 8
TRACERS = GROUPS * PAIR
CELLS = 128
STATE = 128
LISTS = 16
BF = jnp.bfloat16
F32 = jnp.float32
I32 = jnp.int32


def dot(a, b):
    return jnp.dot(a, b, preferred_element_type=F32)


def dot_last(a, b):
    return lax.dot_general(a, b, (((1,), (1,)), ((), ())), preferred_element_type=F32)


def iota(shape, dim):
    return lax.broadcasted_iota(I32, shape, dim)


def spread(codes, slots, rows):
    owner = (iota((slots * rows, CELLS), 0) // rows == iota((slots * rows, CELLS), 1)).astype(BF)
    return dot_last(owner, codes).astype(I32), dot_last(codes, owner).astype(I32)


def write_picks(wanted, rows, left, right, part=slice(None)):
    count = wanted.shape[0]
    hit = jnp.where(wanted == iota((count, STATE), 1), 1.0, 0.0)
    even = iota((count, STATE), 0) // rows % 2 == 0
    left[part] = jnp.where(even, hit, 0.0).astype(BF)
    right[part] = jnp.where(even, 0.0, hit).astype(BF)


def write_place(wanted, place, part=slice(None)):
    shape = (place.shape[0], wanted.shape[1])
    place[:, part] = jnp.where(wanted == iota(shape, 0), 1.0, 0.0).astype(BF)


def level_matrices(codes, row_of, block_of, slots, left, right, place):
    columns, rows = spread(codes, slots, TRACERS)
    tracer = iota((slots * TRACERS, 1), 0) % TRACERS
    wanted = tracer // PAIR * TRACERS + columns[:, row_of : row_of + 1] * PAIR + tracer % PAIR
    write_picks(wanted, TRACERS, left, right)
    tracer = iota((1, slots * TRACERS), 1) % TRACERS
    block = rows[block_of : block_of + 1]
    wanted = block // LEVELS * STATE + tracer // PAIR * TRACERS + block % LEVELS * PAIR + tracer % PAIR
    write_place(jnp.where(block < 0, -1, wanted), place)


def level_products(rows, left, right, place, tiles, first):
    rows = rows.astype(BF)
    x_left = dot(left[...], rows).astype(BF)
    x_right = dot(right[...], rows).astype(BF)
    parts = []
    for at in range(0, left.shape[0] // TRACERS, 4):
        part = slice(at * TRACERS, (at + 4) * TRACERS)
        tile = first + at
        lhs = jnp.concatenate([x_left[part], x_right[part]], axis=1)
        upper = jnp.concatenate([tiles[tile], tiles[tile + 2]], axis=1)
        lower = jnp.concatenate([tiles[tile + 1], tiles[tile + 3]], axis=1)
        out = dot(lhs, jnp.concatenate([upper, lower], axis=0))
        parts += [out[: 2 * TRACERS, :CELLS], out[2 * TRACERS :, CELLS:]]
    return placed(place, jnp.concatenate(parts, axis=0))


def placed(place, product):
    high = product.astype(BF)
    low = (product - high.astype(F32)).astype(BF)
    return dot(place[...], high) + dot(place[...], low)


def open_kernel(
    seed, lengths, l_rows, l_sides, l_targets, l_count, v_rows, v_peers, v_targets, tiles,
    adjoint, partial, wet, left, right, place, codes,
):
    l_slots, v_slots = l_rows.shape[1], v_rows.shape[1]
    codes[...] = jnp.zeros(codes.shape, F32)
    odd = lax.axis_index("region") % 2
    side = jnp.where(odd == 1, 2 - l_sides[...], l_sides[...])
    used = iota((1, l_slots), 1) < l_count[...]
    codes[0:1, 0:l_slots] = l_rows[...].astype(F32)
    codes[1:2, 0:l_slots] = jnp.where(used, side * LEVELS + l_targets[...], -1).astype(F32)
    codes[2:3, 0:v_slots] = v_rows[...].astype(F32)
    codes[3:4, 0:v_slots] = (v_peers[...] * LEVELS + v_targets[...]).astype(F32)
    level = lax.axis_index("depth") * LEVELS + iota((STATE, CELLS), 0) % TRACERS // PAIR
    wet[...] = jnp.where(level < lengths[...], 1.0, 0.0)
    level_matrices(codes[...].astype(BF)[:8], 2, 3, v_slots, left, right, place)
    for group in range(GROUPS):
        for at in range(LEVELS):
            row = group * TRACERS + at * PAIR
            adjoint[row : row + PAIR] = seed[at, group * PAIR : group * PAIR + PAIR]
    value = wet[...] * adjoint[...]
    adjoint[...] = value
    sums = level_products(value, left, right, place, tiles, l_slots).astype(BF)
    for peer in range(GROUPS):
        at = peer * (STATE + LISTS)
        partial[at : at + STATE] = sums[peer * STATE : (peer + 1) * STATE]
        partial[at + STATE : at + STATE + LISTS] = codes[...].astype(BF)


def lateral_lists_kernel(codes, left, right, place):
    level_matrices(codes[...].astype(BF)[:8], 0, 1, left.shape[0] // TRACERS, left, right, place)


def vertical_kernel(base, first, second, wet, left, right, place, tiles, adjoint, partial):
    value = wet[...] * (base[...] + first[...].astype(F32) + second[...].astype(F32))
    adjoint[...] = value
    partial[...] = level_products(value, left, right, place, tiles, tiles.shape[0] - left.shape[0] // TRACERS).astype(BF)


def lateral_kernel(adjoint, returned, wet, left, right, place, tiles, base, to_first, to_second):
    value = adjoint[...]
    stride = returned.shape[0] // GROUPS
    for peer in range(GROUPS):
        value = value + returned[stride * peer : stride * peer + STATE].astype(F32)
    value = wet[...] * value
    partial = level_products(value, left, right, place, tiles, 0).astype(BF)
    to_first[...] = partial[:STATE]
    to_second[...] = partial[2 * STATE :]
    base[...] = value + partial[STATE : 2 * STATE].astype(F32)


def depth_at(place):
    mine = lax.axis_index("depth")
    chip, core = mine // 2, mine % 2
    offset = (0, 3, 1, 2)[place % 4]
    return (chip + offset) % (GROUPS // 2) * 2 + (core if place < 4 else 1 - core)


def tracer_lists_kernel(returned, lengths, wet, v_left, v_right, v_place, l_left, l_right, l_place, lines_l, lines_v):
    level = iota((STATE, CELLS), 0) // PAIR
    wet[...] = jnp.where(level < lengths[...], 1.0, 0.0)
    l_rows, v_rows = l_left.shape[0] // GROUPS, v_left.shape[0] // GROUPS
    stride = STATE + LISTS
    for at in range(GROUPS):
        depth = depth_at(at)
        codes = returned[pl.ds(pl.multiple_of(depth * stride + STATE, LISTS), LISTS)][:8]
        for rows, row_of, left, right in ((l_rows, 0, l_left, l_right), (v_rows, 2, v_left, v_right)):
            columns, lines = spread(codes, rows // PAIR, PAIR)
            part = slice(at * rows, (at + 1) * rows)
            wanted = (depth * LEVELS + columns[:, row_of : row_of + 1]) * PAIR + iota((rows, 1), 0) % PAIR
            write_picks(wanted, PAIR, left, right, part)
            block = lines[row_of + 1 : row_of + 2]
            pair = iota((1, rows), 1) % PAIR
            if row_of == 0:
                wanted = block // LEVELS * STATE + (depth * LEVELS + block % LEVELS) * PAIR + pair
                wanted = jnp.where(block < 0, -1, wanted)
            else:
                wanted = block * PAIR + pair
            line = lines_l if row_of == 0 else lines_v
            line[:, part] = jnp.broadcast_to(wanted, (8, rows))
    write_place(lines_l[0:1], l_place)
    write_place(lines_v[0:1], v_place)


def tracer_products(rows, left, right, place, tiles, first, slots, scratch):
    x_left, x_right, product = scratch
    count = left.shape[0]
    rows = rows.astype(BF)
    x_left[:count] = dot(left[...], rows).astype(BF)
    x_right[:count] = dot(right[...], rows).astype(BF)
    upper_rows = iota((8, CELLS), 0) < 2 * PAIR
    blocks = tiles.shape[0] // GROUPS
    for depth in range(GROUPS):
        for octet in range(slots // 8):
            at = (depth * slots + octet * 8) * PAIR
            part = slice(at, at + 8 * PAIR)
            lhs = jnp.concatenate([x_left[part], x_right[part]], axis=1)
            for quad in range(2):
                tile = depth * blocks + first + octet * 8 + quad * 4
                upper = jnp.concatenate([tiles[tile], tiles[tile + 2]], axis=1)
                lower = jnp.concatenate([tiles[tile + 1], tiles[tile + 3]], axis=1)
                out = dot(lhs, jnp.concatenate([upper, lower], axis=0))[8 * quad : 8 * quad + 8]
                product[at + 8 * quad : at + 8 * quad + 8] = jnp.where(upper_rows, out[:, :CELLS], out[:, CELLS:])
    return placed(place, product[:count])


def tracer_step(value, wet, v_left, v_right, v_place, l_left, l_right, l_place, tiles, *refs):
    (base, to_first, to_second), scratch = refs[:3], refs[4:]
    l_slots, v_slots = l_left.shape[0] // (GROUPS * PAIR), v_left.shape[0] // (GROUPS * PAIR)
    value = wet[...] * value
    value = wet[...] * (value + tracer_products(value, v_left, v_right, v_place, tiles, l_slots, v_slots, scratch))
    partial = tracer_products(value, l_left, l_right, l_place, tiles, 0, l_slots, scratch)
    to_first[...] = partial[:STATE].astype(BF)
    to_second[...] = partial[2 * STATE :].astype(BF)
    base[...] = value + partial[STATE : 2 * STATE]


def tracer_first_kernel(value, *refs):
    constants, parts, (base, to_first, to_second, tiles) = refs[:7], refs[7:13], refs[13:17]
    *scratch, done = refs[17:]
    copies, at = [], 0
    for index, part in enumerate(parts):
        count = part.shape[0]
        copies.append(pltpu.make_async_copy(part, tiles.at[pl.ds(at, count)], done.at[index]))
        copies[-1].start()
        at += count
    for copy in copies:
        copy.wait()
    tracer_step(value[...], *constants, tiles, base, to_first, to_second, tiles, *scratch)


def tracer_kernel(base, first, second, *refs):
    tracer_step(base[...] + first[...].astype(F32) + second[...].astype(F32), *refs)


def sum_kernel(base, first, second, total):
    total[...] = base[...] + first[...].astype(F32) + second[...].astype(F32)


def close_kernel(value, wet, out):
    rows = wet[...] * value[...]
    for group in range(GROUPS):
        for at in range(LEVELS):
            row = group * TRACERS + at * PAIR
            out[at, group * PAIR : group * PAIR + PAIR] = rows[row : row + PAIR]


def call(body, outs, *args, scratch=(), mebibytes=12, parts=0, kept=None):
    aliases = {} if kept is None else {kept: len(outs) - 1}
    spaces = [pltpu.VMEM] * (len(args) - parts) + [pl.ANY] * parts
    shapes = [jax.ShapeDtypeStruct(shape, kind) for shape, kind in outs]
    if parts or kept is not None:
        shapes[-1] = pltpu.VMEM(*outs[-1])
    return pl.pallas_call(
        body,
        out_shape=shapes,
        input_output_aliases=aliases,
        in_specs=[pl.BlockSpec(memory_space=space) for space in spaces],
        out_specs=[pl.BlockSpec(memory_space=pltpu.VMEM) for _ in outs],
        scratch_shapes=scratch,
        compiler_params=pltpu.CompilerParams(vmem_limit_bytes=mebibytes * 1024 * 1024),
    )(*args)


def swapped(to_first, to_second):
    regions = lax.axis_size("region")
    first = [(i, (i + 1) % regions if i % 2 else (i - 1) % regions) for i in range(regions)]
    second = [(i, i ^ 1) for i in range(regions)]
    from_first = lax.ppermute(to_first, "region", first)
    from_second = lax.ppermute(to_second, "region", second)
    return from_first, from_second


def join_kernel(*refs):
    out, at = refs[-1], 0
    for part in refs[:-1]:
        out[at : at + part.shape[0]] = part[...]
        at += part.shape[0]


def joined(*parts):
    count = sum(part.shape[0] for part in parts)
    return call(join_kernel, [((count, CELLS, CELLS), BF)], *parts, mebibytes=20)[0]


def from_chip(value, by):
    depths = lax.axis_size("depth")
    return lax.ppermute(value, "depth", [(i, (i + 2 * by) % depths) for i in range(depths)])


def from_core(value):
    return lax.ppermute(value, "depth", [(i, i ^ 1) for i in range(lax.axis_size("depth"))])


def to_depth(value):
    return lax.all_to_all(value, "depth", split_axis=0, concat_axis=0, tiled=True)


def local(
    adjoint_seed,
    column_lengths,
    lateral_tiles,
    lateral_rows,
    lateral_sides,
    lateral_targets,
    lateral_counts,
    vertical_tiles,
    vertical_rows,
    vertical_peers,
    vertical_targets,
):
    own = joined(lateral_tiles, vertical_tiles)
    half = own.shape[0] // 2
    before, after = from_chip(own, 1), from_chip(own, -1)
    l_slots, v_slots = lateral_tiles.shape[0], vertical_tiles.shape[0]
    lengths = column_lengths.reshape(1, CELLS)
    state = ((STATE, CELLS), F32)
    sent = ((STATE, CELLS), BF)

    def matrices(slots, blocks):
        return [((slots * TRACERS, STATE), BF)] * 2 + [((blocks * STATE, slots * TRACERS), BF)]

    adjoint, partial, wet, *vertical, codes = call(
        open_kernel,
        [state, ((GROUPS * (STATE + LISTS), CELLS), BF), state]
        + matrices(v_slots, GROUPS)
        + [((LISTS, CELLS), F32)],
        adjoint_seed,
        lengths,
        lateral_rows.reshape(1, l_slots),
        lateral_sides.reshape(1, l_slots),
        lateral_targets.reshape(1, l_slots),
        lateral_counts,
        vertical_rows.reshape(1, v_slots),
        vertical_peers.reshape(1, v_slots),
        vertical_targets.reshape(1, v_slots),
        own,
    )
    lateral = call(lateral_lists_kernel, matrices(l_slots, 3), codes)
    returned = first_returned = to_depth(partial)
    for step in range(LEVEL_STEPS):
        if step == LEVEL_STEPS - 1:
            returned, opposite = lax.optimization_barrier((returned, opposite))
            opposite = joined(*opposite)
            swapped_opposite = from_core(opposite)
        base, to_first, to_second = call(
            lateral_kernel, [state, sent, sent], adjoint, returned, wet, *lateral, own
        )
        received = swapped(to_first, to_second)
        if step == LEVEL_STEPS - 2:
            received, before, after = lax.optimization_barrier((received, before, after))
            opposite = from_chip(before[:half], 1), from_chip(after[half:], -1)
            three = joined(own, before, after)
            swapped_three = from_core(three)
        if step < LEVEL_STEPS - 1:
            adjoint, partial = call(
                vertical_kernel, [state, ((GROUPS * STATE, CELLS), BF)], base, *received, wet, *vertical, own
            )
            returned = to_depth(partial)
    parts = (own, before, after, opposite, swapped_three, swapped_opposite)

    def tracer_matrices(slots, blocks):
        rows = slots * PAIR
        return [((GROUPS * rows, STATE), BF)] * 2 + [((blocks * STATE, GROUPS * rows), BF)]

    constants = call(
        tracer_lists_kernel,
        [state] + tracer_matrices(v_slots, 1) + tracer_matrices(l_slots, 3),
        first_returned,
        lengths,
        scratch=[pltpu.VMEM((8, GROUPS * slots * PAIR), I32) for slots in (l_slots, v_slots)],
    )
    rows = GROUPS * l_slots * PAIR
    scratch = [pltpu.VMEM((rows, CELLS), kind) for kind in (BF, BF, F32)]
    (value,) = call(sum_kernel, [state], base, *received)
    value = to_depth(value)
    held = ((GROUPS * own.shape[0], CELLS, CELLS), BF)
    outs = [state, sent, sent, held]
    for step in range(LEVEL_STEPS, STEPS):
        if step == LEVEL_STEPS:
            base, to_first, to_second, tiles = call(
                tracer_first_kernel,
                outs,
                value,
                *constants,
                *parts,
                scratch=scratch + [pltpu.SemaphoreType.DMA((len(parts),))],
                mebibytes=24,
                parts=len(parts),
            )
        else:
            base, to_first, to_second, tiles = call(
                tracer_kernel,
                outs,
                base,
                *received,
                *constants,
                tiles,
                scratch=scratch,
                mebibytes=24,
                kept=3 + len(constants),
            )
        received = swapped(to_first, to_second)
    (value,) = call(sum_kernel, [state], base, *received)
    (adjoint,) = call(close_kernel, [((LEVELS, TRACERS, CELLS), F32)], to_depth(value), wet)
    return adjoint


def solution(mesh):
    return jax.shard_map(
        local,
        mesh=mesh,
        in_specs=(
            P("depth", None, "region"),
            P("region"),
            P("depth", "region", None),
            P("depth", "region"),
            P("depth", "region"),
            P("depth", "region"),
            P("depth", "region"),
            P("depth", "region", None),
            P("depth", "region"),
            P("depth", "region"),
            P("depth", "region"),
        ),
        out_specs=P("depth", None, "region"),
        check_vma=False,
    )
```

```python
import jax
import jax.numpy as jnp
from jax import lax
from jax.experimental import pallas as pl
from jax.experimental.pallas import tpu as pltpu
from jax.sharding import PartitionSpec as P

STEPS = 12
LEVEL_STEPS = 3
GROUPS = 8
PAIR = 2
LEVELS = 8
TRACERS = GROUPS * PAIR
CELLS = 128
STATE = 128
LISTS = 16
BF = jnp.bfloat16
F32 = jnp.float32
I32 = jnp.int32


def dot(a, b):
    return jnp.dot(a, b, preferred_element_type=F32)


def dot_last(a, b):
    return lax.dot_general(a, b, (((1,), (1,)), ((), ())), preferred_element_type=F32)


def iota(shape, dim):
    return lax.broadcasted_iota(I32, shape, dim)


def spread(codes, slots, rows):
    owner = (iota((slots * rows, CELLS), 0) // rows == iota((slots * rows, CELLS), 1)).astype(BF)
    return dot_last(owner, codes).astype(I32), dot_last(codes, owner).astype(I32)


def write_picks(wanted, rows, left, right, part=slice(None)):
    count = wanted.shape[0]
    hit = jnp.where(wanted == iota((count, STATE), 1), 1.0, 0.0)
    even = iota((count, STATE), 0) // rows % 2 == 0
    left[part] = jnp.where(even, hit, 0.0).astype(BF)
    right[part] = jnp.where(even, 0.0, hit).astype(BF)


def write_place(wanted, place, part=slice(None)):
    shape = (place.shape[0], wanted.shape[1])
    place[:, part] = jnp.where(wanted == iota(shape, 0), 1.0, 0.0).astype(BF)


def level_matrices(codes, row_of, block_of, slots, left, right, place):
    columns, rows = spread(codes, slots, TRACERS)
    tracer = iota((slots * TRACERS, 1), 0) % TRACERS
    wanted = tracer // PAIR * TRACERS + columns[:, row_of : row_of + 1] * PAIR + tracer % PAIR
    write_picks(wanted, TRACERS, left, right)
    tracer = iota((1, slots * TRACERS), 1) % TRACERS
    block = rows[block_of : block_of + 1]
    wanted = block // LEVELS * STATE + tracer // PAIR * TRACERS + block % LEVELS * PAIR + tracer % PAIR
    write_place(jnp.where(block < 0, -1, wanted), place)


def level_products(rows, left, right, place, tiles):
    rows = rows.astype(BF)
    x_left = dot(left[...], rows).astype(BF)
    x_right = dot(right[...], rows).astype(BF)
    parts = []
    for at in range(0, tiles.shape[0], 4):
        part = slice(at * TRACERS, (at + 4) * TRACERS)
        lhs = jnp.concatenate([x_left[part], x_right[part]], axis=1)
        upper = jnp.concatenate([tiles[at], tiles[at + 2]], axis=1)
        lower = jnp.concatenate([tiles[at + 1], tiles[at + 3]], axis=1)
        out = dot(lhs, jnp.concatenate([upper, lower], axis=0))
        parts += [out[: 2 * TRACERS, :CELLS], out[2 * TRACERS :, CELLS:]]
    return placed(place, jnp.concatenate(parts, axis=0))


def placed(place, product):
    high = product.astype(BF)
    low = (product - high.astype(F32)).astype(BF)
    return dot(place[...], high) + dot(place[...], low)


def open_kernel(
    seed, lengths, l_rows, l_sides, l_targets, l_count, v_rows, v_peers, v_targets, tiles,
    adjoint, partial, wet, left, right, place, codes,
):
    l_slots, v_slots = l_rows.shape[1], v_rows.shape[1]
    codes[...] = jnp.zeros(codes.shape, F32)
    odd = lax.axis_index("region") % 2
    side = jnp.where(odd == 1, 2 - l_sides[...], l_sides[...])
    used = iota((1, l_slots), 1) < l_count[...]
    codes[0:1, 0:l_slots] = l_rows[...].astype(F32)
    codes[1:2, 0:l_slots] = jnp.where(used, side * LEVELS + l_targets[...], -1).astype(F32)
    codes[2:3, 0:v_slots] = v_rows[...].astype(F32)
    codes[3:4, 0:v_slots] = (v_peers[...] * LEVELS + v_targets[...]).astype(F32)
    level = lax.axis_index("depth") * LEVELS + iota((STATE, CELLS), 0) % TRACERS // PAIR
    wet[...] = jnp.where(level < lengths[...], 1.0, 0.0)
    level_matrices(codes[...].astype(BF)[:8], 2, 3, v_slots, left, right, place)
    for group in range(GROUPS):
        for at in range(LEVELS):
            row = group * TRACERS + at * PAIR
            adjoint[row : row + PAIR] = seed[at, group * PAIR : group * PAIR + PAIR]
    value = wet[...] * adjoint[...]
    adjoint[...] = value
    sums = level_products(value, left, right, place, tiles).astype(BF)
    for peer in range(GROUPS):
        at = peer * (STATE + LISTS)
        partial[at : at + STATE] = sums[peer * STATE : (peer + 1) * STATE]
        partial[at + STATE : at + STATE + LISTS] = codes[...].astype(BF)


def lateral_lists_kernel(codes, left, right, place):
    level_matrices(codes[...].astype(BF)[:8], 0, 1, left.shape[0] // TRACERS, left, right, place)


def vertical_kernel(base, first, second, wet, left, right, place, tiles, adjoint, partial):
    value = wet[...] * (base[...] + first[...].astype(F32) + second[...].astype(F32))
    adjoint[...] = value
    partial[...] = level_products(value, left, right, place, tiles).astype(BF)


def lateral_kernel(adjoint, returned, wet, left, right, place, tiles, base, to_first, to_second):
    value = adjoint[...]
    stride = returned.shape[0] // GROUPS
    for peer in range(GROUPS):
        value = value + returned[stride * peer : stride * peer + STATE].astype(F32)
    value = wet[...] * value
    partial = level_products(value, left, right, place, tiles).astype(BF)
    to_first[...] = partial[:STATE]
    to_second[...] = partial[2 * STATE :]
    base[...] = value + partial[STATE : 2 * STATE].astype(F32)


def tracer_lists_kernel(returned, lengths, wet, v_left, v_right, v_place, l_left, l_right, l_place, lines_l, lines_v):
    level = iota((STATE, CELLS), 0) // PAIR
    wet[...] = jnp.where(level < lengths[...], 1.0, 0.0)
    l_rows, v_rows = l_left.shape[0] // GROUPS, v_left.shape[0] // GROUPS
    stride = STATE + LISTS
    for depth in range(GROUPS):
        codes = returned[depth * stride + STATE : (depth + 1) * stride][:8]
        for rows, row_of, left, right in ((l_rows, 0, l_left, l_right), (v_rows, 2, v_left, v_right)):
            columns, lines = spread(codes, rows // PAIR, PAIR)
            part = slice(depth * rows, (depth + 1) * rows)
            wanted = (depth * LEVELS + columns[:, row_of : row_of + 1]) * PAIR + iota((rows, 1), 0) % PAIR
            write_picks(wanted, PAIR, left, right, part)
            block = lines[row_of + 1 : row_of + 2]
            pair = iota((1, rows), 1) % PAIR
            if row_of == 0:
                wanted = block // LEVELS * STATE + (depth * LEVELS + block % LEVELS) * PAIR + pair
                wanted = jnp.where(block < 0, -1, wanted)
            else:
                wanted = block * PAIR + pair
            line = lines_l if row_of == 0 else lines_v
            line[:, part] = jnp.broadcast_to(wanted, (8, rows))
    write_place(lines_l[0:1], l_place)
    write_place(lines_v[0:1], v_place)


def tracer_products(rows, left, right, place, tiles, first, slots, scratch):
    x_left, x_right, product = scratch
    count = left.shape[0]
    rows = rows.astype(BF)
    x_left[:count] = dot(left[...], rows).astype(BF)
    x_right[:count] = dot(right[...], rows).astype(BF)
    upper_rows = iota((8, CELLS), 0) < 2 * PAIR
    blocks = tiles.shape[0] // GROUPS
    for depth in range(GROUPS):
        for octet in range(slots // 8):
            at = (depth * slots + octet * 8) * PAIR
            part = slice(at, at + 8 * PAIR)
            lhs = jnp.concatenate([x_left[part], x_right[part]], axis=1)
            for quad in range(2):
                tile = depth * blocks + first + octet * 8 + quad * 4
                upper = jnp.concatenate([tiles[tile], tiles[tile + 2]], axis=1)
                lower = jnp.concatenate([tiles[tile + 1], tiles[tile + 3]], axis=1)
                out = dot(lhs, jnp.concatenate([upper, lower], axis=0))[8 * quad : 8 * quad + 8]
                product[at + 8 * quad : at + 8 * quad + 8] = jnp.where(upper_rows, out[:, :CELLS], out[:, CELLS:])
    return placed(place, product[:count])


def tracer_step(value, wet, v_left, v_right, v_place, l_left, l_right, l_place, tiles, base, to_first, to_second, *scratch):
    l_slots, v_slots = l_left.shape[0] // (GROUPS * PAIR), v_left.shape[0] // (GROUPS * PAIR)
    value = wet[...] * value
    value = wet[...] * (value + tracer_products(value, v_left, v_right, v_place, tiles, l_slots, v_slots, scratch))
    partial = tracer_products(value, l_left, l_right, l_place, tiles, 0, l_slots, scratch)
    to_first[...] = partial[:STATE].astype(BF)
    to_second[...] = partial[2 * STATE :].astype(BF)
    base[...] = value + partial[STATE : 2 * STATE]


def tracer_first_kernel(value, *refs):
    tracer_step(value[...], *refs)


def tracer_kernel(base, first, second, *refs):
    tracer_step(base[...] + first[...].astype(F32) + second[...].astype(F32), *refs)


def sum_kernel(base, first, second, total):
    total[...] = base[...] + first[...].astype(F32) + second[...].astype(F32)


def close_kernel(value, wet, out):
    rows = wet[...] * value[...]
    for group in range(GROUPS):
        for at in range(LEVELS):
            row = group * TRACERS + at * PAIR
            out[at, group * PAIR : group * PAIR + PAIR] = rows[row : row + PAIR]


def call(body, outs, *args, scratch=()):
    return pl.pallas_call(
        body,
        out_shape=[jax.ShapeDtypeStruct(shape, kind) for shape, kind in outs],
        in_specs=[pl.BlockSpec(memory_space=pltpu.VMEM) for _ in args],
        out_specs=[pl.BlockSpec(memory_space=pltpu.VMEM) for _ in outs],
        scratch_shapes=scratch,
        compiler_params=pltpu.CompilerParams(vmem_limit_bytes=24 * 1024 * 1024),
    )(*args)


def swapped(to_first, to_second):
    regions = lax.axis_size("region")
    first = [(i, (i + 1) % regions if i % 2 else (i - 1) % regions) for i in range(regions)]
    second = [(i, i ^ 1) for i in range(regions)]
    from_first = lax.ppermute(to_first, "region", first)
    from_second = lax.ppermute(to_second, "region", second)
    return from_first, from_second


def to_depth(value):
    return lax.all_to_all(value, "depth", split_axis=0, concat_axis=0, tiled=True)


def local(
    adjoint_seed,
    column_lengths,
    lateral_tiles,
    lateral_rows,
    lateral_sides,
    lateral_targets,
    lateral_counts,
    vertical_tiles,
    vertical_rows,
    vertical_peers,
    vertical_targets,
):
    gathered = lax.all_gather(
        jnp.concatenate([lateral_tiles, vertical_tiles], axis=0), "depth", axis=0, tiled=True
    )
    l_slots, v_slots = lateral_tiles.shape[0], vertical_tiles.shape[0]
    lengths = column_lengths.reshape(1, CELLS)
    state = ((STATE, CELLS), F32)
    sent = ((STATE, CELLS), BF)

    def matrices(slots, blocks):
        return [((slots * TRACERS, STATE), BF)] * 2 + [((blocks * STATE, slots * TRACERS), BF)]

    adjoint, partial, wet, *vertical, codes = call(
        open_kernel,
        [state, ((GROUPS * (STATE + LISTS), CELLS), BF), state]
        + matrices(v_slots, GROUPS)
        + [((LISTS, CELLS), F32)],
        adjoint_seed,
        lengths,
        lateral_rows.reshape(1, l_slots),
        lateral_sides.reshape(1, l_slots),
        lateral_targets.reshape(1, l_slots),
        lateral_counts,
        vertical_rows.reshape(1, v_slots),
        vertical_peers.reshape(1, v_slots),
        vertical_targets.reshape(1, v_slots),
        vertical_tiles,
    )
    lateral = call(lateral_lists_kernel, matrices(l_slots, 3), codes)
    returned = first_returned = to_depth(partial)
    for step in range(LEVEL_STEPS):
        base, to_first, to_second = call(
            lateral_kernel, [state, sent, sent], adjoint, returned, wet, *lateral, lateral_tiles
        )
        received = swapped(to_first, to_second)
        if step < LEVEL_STEPS - 1:
            adjoint, partial = call(
                vertical_kernel,
                [state, ((GROUPS * STATE, CELLS), BF)],
                base,
                *received,
                wet,
                *vertical,
                vertical_tiles,
            )
            returned = to_depth(partial)

    def tracer_matrices(slots, blocks):
        rows = slots * PAIR
        return [((GROUPS * rows, STATE), BF)] * 2 + [((blocks * STATE, GROUPS * rows), BF)]

    constants = call(
        tracer_lists_kernel,
        [state] + tracer_matrices(v_slots, 1) + tracer_matrices(l_slots, 3),
        first_returned,
        lengths,
        scratch=[pltpu.VMEM((8, GROUPS * slots * PAIR), I32) for slots in (l_slots, v_slots)],
    )
    rows = GROUPS * l_slots * PAIR
    scratch = [pltpu.VMEM((rows, CELLS), kind) for kind in (BF, BF, F32)]
    (value,) = call(sum_kernel, [state], base, *received)
    value = to_depth(value)
    for step in range(LEVEL_STEPS, STEPS):
        if step == LEVEL_STEPS:
            arrived, body = (value,), tracer_first_kernel
        else:
            arrived, body = (base, *received), tracer_kernel
        base, to_first, to_second = call(body, [state, sent, sent], *arrived, *constants, gathered, scratch=scratch)
        received = swapped(to_first, to_second)
    (value,) = call(sum_kernel, [state], base, *received)
    (adjoint,) = call(close_kernel, [((LEVELS, TRACERS, CELLS), F32)], to_depth(value), wet)
    return adjoint


def solution(mesh):
    return jax.shard_map(
        local,
        mesh=mesh,
        in_specs=(
            P("depth", None, "region"),
            P("region"),
            P("depth", "region", None),
            P("depth", "region"),
            P("depth", "region"),
            P("depth", "region"),
            P("depth", "region"),
            P("depth", "region", None),
            P("depth", "region"),
            P("depth", "region"),
            P("depth", "region"),
        ),
        out_specs=P("depth", None, "region"),
        check_vma=False,
    )
```

```python
import jax
import jax.numpy as jnp
from jax import lax
from jax.experimental import pallas as pl
from jax.experimental.pallas import tpu as pltpu
from jax.sharding import PartitionSpec as P

STEPS = 12
LEVEL_STEPS = 3
GROUPS = 8
PAIR = 2
LEVELS = 8
TRACERS = GROUPS * PAIR
CELLS = 128
STATE = 128
LISTS = 16
BF = jnp.bfloat16
F32 = jnp.float32
I32 = jnp.int32


def dot(a, b):
    return jnp.dot(a, b, preferred_element_type=F32)


def dot_last(a, b):
    return lax.dot_general(a, b, (((1,), (1,)), ((), ())), preferred_element_type=F32)


def iota(shape, dim):
    return lax.broadcasted_iota(I32, shape, dim)


def spread(codes, slots, rows):
    owner = (iota((slots * rows, CELLS), 0) // rows == iota((slots * rows, CELLS), 1)).astype(BF)
    return dot_last(owner, codes).astype(I32), dot_last(codes, owner).astype(I32)


def write_picks(wanted, rows, left, right, part=slice(None)):
    count = wanted.shape[0]
    hit = jnp.where(wanted == iota((count, STATE), 1), 1.0, 0.0)
    even = iota((count, STATE), 0) // rows % 2 == 0
    left[part] = jnp.where(even, hit, 0.0).astype(BF)
    right[part] = jnp.where(even, 0.0, hit).astype(BF)


def write_place(wanted, place, part=slice(None)):
    shape = (place.shape[0], wanted.shape[1])
    place[:, part] = jnp.where(wanted == iota(shape, 0), 1.0, 0.0).astype(BF)


def level_matrices(codes, row_of, block_of, slots, left, right, place):
    columns, rows = spread(codes, slots, TRACERS)
    tracer = iota((slots * TRACERS, 1), 0) % TRACERS
    wanted = tracer // PAIR * TRACERS + columns[:, row_of : row_of + 1] * PAIR + tracer % PAIR
    write_picks(wanted, TRACERS, left, right)
    tracer = iota((1, slots * TRACERS), 1) % TRACERS
    block = rows[block_of : block_of + 1]
    wanted = block // LEVELS * STATE + tracer // PAIR * TRACERS + block % LEVELS * PAIR + tracer % PAIR
    write_place(jnp.where(block < 0, -1, wanted), place)


def level_products(rows, left, right, place, tiles):
    rows = rows.astype(BF)
    x_left = dot(left[...], rows).astype(BF)
    x_right = dot(right[...], rows).astype(BF)
    parts = []
    for at in range(0, tiles.shape[0], 4):
        part = slice(at * TRACERS, (at + 4) * TRACERS)
        lhs = jnp.concatenate([x_left[part], x_right[part]], axis=1)
        upper = jnp.concatenate([tiles[at], tiles[at + 2]], axis=1)
        lower = jnp.concatenate([tiles[at + 1], tiles[at + 3]], axis=1)
        out = dot(lhs, jnp.concatenate([upper, lower], axis=0))
        parts += [out[: 2 * TRACERS, :CELLS], out[2 * TRACERS :, CELLS:]]
    return placed(place, jnp.concatenate(parts, axis=0))


def placed(place, product):
    high = product.astype(BF)
    low = (product - high.astype(F32)).astype(BF)
    return dot(place[...], high) + dot(place[...], low)


def open_kernel(
    seed, lengths, l_rows, l_sides, l_targets, l_count, v_rows, v_peers, v_targets, tiles,
    adjoint, partial, wet, left, right, place, codes,
):
    l_slots, v_slots = l_rows.shape[1], v_rows.shape[1]
    codes[...] = jnp.zeros(codes.shape, F32)
    odd = lax.axis_index("region") % 2
    side = jnp.where(odd == 1, 2 - l_sides[...], l_sides[...])
    used = iota((1, l_slots), 1) < l_count[...]
    codes[0:1, 0:l_slots] = l_rows[...].astype(F32)
    codes[1:2, 0:l_slots] = jnp.where(used, side * LEVELS + l_targets[...], -1).astype(F32)
    codes[2:3, 0:v_slots] = v_rows[...].astype(F32)
    codes[3:4, 0:v_slots] = (v_peers[...] * LEVELS + v_targets[...]).astype(F32)
    level = lax.axis_index("depth") * LEVELS + iota((STATE, CELLS), 0) % TRACERS // PAIR
    wet[...] = jnp.where(level < lengths[...], 1.0, 0.0)
    level_matrices(codes[...].astype(BF)[:8], 2, 3, v_slots, left, right, place)
    for group in range(GROUPS):
        for at in range(LEVELS):
            row = group * TRACERS + at * PAIR
            adjoint[row : row + PAIR] = seed[at, group * PAIR : group * PAIR + PAIR]
    value = wet[...] * adjoint[...]
    adjoint[...] = value
    sums = level_products(value, left, right, place, tiles).astype(BF)
    for peer in range(GROUPS):
        at = peer * (STATE + LISTS)
        partial[at : at + STATE] = sums[peer * STATE : (peer + 1) * STATE]
        partial[at + STATE : at + STATE + LISTS] = codes[...].astype(BF)


def lateral_lists_kernel(codes, left, right, place):
    level_matrices(codes[...].astype(BF)[:8], 0, 1, left.shape[0] // TRACERS, left, right, place)


def vertical_kernel(base, first, second, wet, left, right, place, tiles, adjoint, partial):
    value = wet[...] * (base[...] + first[...].astype(F32) + second[...].astype(F32))
    adjoint[...] = value
    partial[...] = level_products(value, left, right, place, tiles).astype(BF)


def lateral_kernel(adjoint, returned, wet, left, right, place, tiles, base, to_first, to_second):
    value = adjoint[...]
    stride = returned.shape[0] // GROUPS
    for peer in range(GROUPS):
        value = value + returned[stride * peer : stride * peer + STATE].astype(F32)
    value = wet[...] * value
    partial = level_products(value, left, right, place, tiles).astype(BF)
    to_first[...] = partial[:STATE]
    to_second[...] = partial[2 * STATE :]
    base[...] = value + partial[STATE : 2 * STATE].astype(F32)


def tracer_lists_kernel(returned, lengths, wet, v_left, v_right, v_place, l_left, l_right, l_place, lines_l, lines_v):
    level = iota((STATE, CELLS), 0) // PAIR
    wet[...] = jnp.where(level < lengths[...], 1.0, 0.0)
    l_rows, v_rows = l_left.shape[0] // GROUPS, v_left.shape[0] // GROUPS
    stride = STATE + LISTS
    for depth in range(GROUPS):
        codes = returned[depth * stride + STATE : (depth + 1) * stride][:8]
        for rows, row_of, left, right in ((l_rows, 0, l_left, l_right), (v_rows, 2, v_left, v_right)):
            columns, lines = spread(codes, rows // PAIR, PAIR)
            part = slice(depth * rows, (depth + 1) * rows)
            wanted = (depth * LEVELS + columns[:, row_of : row_of + 1]) * PAIR + iota((rows, 1), 0) % PAIR
            write_picks(wanted, PAIR, left, right, part)
            block = lines[row_of + 1 : row_of + 2]
            pair = iota((1, rows), 1) % PAIR
            if row_of == 0:
                wanted = block // LEVELS * STATE + (depth * LEVELS + block % LEVELS) * PAIR + pair
                wanted = jnp.where(block < 0, -1, wanted)
            else:
                wanted = block * PAIR + pair
            line = lines_l if row_of == 0 else lines_v
            line[:, part] = jnp.broadcast_to(wanted, (8, rows))
    write_place(lines_l[0:1], l_place)
    write_place(lines_v[0:1], v_place)


def tracer_products(rows, left, right, place, tiles, slots, scratch):
    x_left, x_right, product = scratch
    count = left.shape[0]
    rows = rows.astype(BF)
    x_left[:count] = dot(left[...], rows).astype(BF)
    x_right[:count] = dot(right[...], rows).astype(BF)
    upper_rows = iota((8, CELLS), 0) < 2 * PAIR
    for depth in range(GROUPS):
        for octet in range(slots // 8):
            at = (depth * slots + octet * 8) * PAIR
            part = slice(at, at + 8 * PAIR)
            lhs = jnp.concatenate([x_left[part], x_right[part]], axis=1)
            for quad in range(2):
                tile = depth * slots + octet * 8 + quad * 4
                upper = jnp.concatenate([tiles[tile], tiles[tile + 2]], axis=1)
                lower = jnp.concatenate([tiles[tile + 1], tiles[tile + 3]], axis=1)
                out = dot(lhs, jnp.concatenate([upper, lower], axis=0))[8 * quad : 8 * quad + 8]
                product[at + 8 * quad : at + 8 * quad + 8] = jnp.where(upper_rows, out[:, :CELLS], out[:, CELLS:])
    return placed(place, product[:count])


def tracer_step(
    value, wet, v_left, v_right, v_place, l_left, l_right, l_place, v_tiles, l_tiles,
    base, to_first, to_second, *scratch,
):
    l_slots, v_slots = l_left.shape[0] // (GROUPS * PAIR), v_left.shape[0] // (GROUPS * PAIR)
    value = wet[...] * value
    value = wet[...] * (value + tracer_products(value, v_left, v_right, v_place, v_tiles, v_slots, scratch))
    partial = tracer_products(value, l_left, l_right, l_place, l_tiles, l_slots, scratch)
    to_first[...] = partial[:STATE].astype(BF)
    to_second[...] = partial[2 * STATE :].astype(BF)
    base[...] = value + partial[STATE : 2 * STATE]


def tracer_first_kernel(value, *refs):
    tracer_step(value[...], *refs)


def tracer_kernel(base, first, second, *refs):
    tracer_step(base[...] + first[...].astype(F32) + second[...].astype(F32), *refs)


def sum_kernel(base, first, second, total):
    total[...] = base[...] + first[...].astype(F32) + second[...].astype(F32)


def close_kernel(value, wet, out):
    rows = wet[...] * value[...]
    for group in range(GROUPS):
        for at in range(LEVELS):
            row = group * TRACERS + at * PAIR
            out[at, group * PAIR : group * PAIR + PAIR] = rows[row : row + PAIR]


def call(body, outs, *args, scratch=()):
    return pl.pallas_call(
        body,
        out_shape=[jax.ShapeDtypeStruct(shape, kind) for shape, kind in outs],
        in_specs=[pl.BlockSpec(memory_space=pltpu.VMEM) for _ in args],
        out_specs=[pl.BlockSpec(memory_space=pltpu.VMEM) for _ in outs],
        scratch_shapes=scratch,
        compiler_params=pltpu.CompilerParams(vmem_limit_bytes=24 * 1024 * 1024),
    )(*args)


def swapped(to_first, to_second):
    regions = lax.axis_size("region")
    first = [(i, (i + 1) % regions if i % 2 else (i - 1) % regions) for i in range(regions)]
    second = [(i, i ^ 1) for i in range(regions)]
    from_first = lax.ppermute(to_first, "region", first)
    from_second = lax.ppermute(to_second, "region", second)
    return from_first, from_second


def to_depth(value):
    return lax.all_to_all(value, "depth", split_axis=0, concat_axis=0, tiled=True)


def local(
    adjoint_seed,
    column_lengths,
    lateral_tiles,
    lateral_rows,
    lateral_sides,
    lateral_targets,
    lateral_counts,
    vertical_tiles,
    vertical_rows,
    vertical_peers,
    vertical_targets,
):
    gathered = [
        lax.all_gather(tiles, "depth", axis=0, tiled=True) for tiles in (vertical_tiles, lateral_tiles)
    ]
    l_slots, v_slots = lateral_tiles.shape[0], vertical_tiles.shape[0]
    lengths = column_lengths.reshape(1, CELLS)
    state = ((STATE, CELLS), F32)
    sent = ((STATE, CELLS), BF)

    def matrices(slots, blocks):
        return [((slots * TRACERS, STATE), BF)] * 2 + [((blocks * STATE, slots * TRACERS), BF)]

    adjoint, partial, wet, *vertical, codes = call(
        open_kernel,
        [state, ((GROUPS * (STATE + LISTS), CELLS), BF), state]
        + matrices(v_slots, GROUPS)
        + [((LISTS, CELLS), F32)],
        adjoint_seed,
        lengths,
        lateral_rows.reshape(1, l_slots),
        lateral_sides.reshape(1, l_slots),
        lateral_targets.reshape(1, l_slots),
        lateral_counts,
        vertical_rows.reshape(1, v_slots),
        vertical_peers.reshape(1, v_slots),
        vertical_targets.reshape(1, v_slots),
        vertical_tiles,
    )
    lateral = call(lateral_lists_kernel, matrices(l_slots, 3), codes)
    returned = first_returned = to_depth(partial)
    for step in range(LEVEL_STEPS):
        base, to_first, to_second = call(
            lateral_kernel, [state, sent, sent], adjoint, returned, wet, *lateral, lateral_tiles
        )
        received = swapped(to_first, to_second)
        if step < LEVEL_STEPS - 1:
            adjoint, partial = call(
                vertical_kernel,
                [state, ((GROUPS * STATE, CELLS), BF)],
                base,
                *received,
                wet,
                *vertical,
                vertical_tiles,
            )
            returned = to_depth(partial)

    def tracer_matrices(slots, blocks):
        rows = slots * PAIR
        return [((GROUPS * rows, STATE), BF)] * 2 + [((blocks * STATE, GROUPS * rows), BF)]

    constants = call(
        tracer_lists_kernel,
        [state] + tracer_matrices(v_slots, 1) + tracer_matrices(l_slots, 3),
        first_returned,
        lengths,
        scratch=[pltpu.VMEM((8, GROUPS * slots * PAIR), I32) for slots in (l_slots, v_slots)],
    )
    rows = GROUPS * l_slots * PAIR
    scratch = [pltpu.VMEM((rows, CELLS), kind) for kind in (BF, BF, F32)]
    (value,) = call(sum_kernel, [state], base, *received)
    value = to_depth(value)
    for step in range(LEVEL_STEPS, STEPS):
        if step == LEVEL_STEPS:
            arrived, body = (value,), tracer_first_kernel
        else:
            arrived, body = (base, *received), tracer_kernel
        base, to_first, to_second = call(body, [state, sent, sent], *arrived, *constants, *gathered, scratch=scratch)
        received = swapped(to_first, to_second)
    (value,) = call(sum_kernel, [state], base, *received)
    (adjoint,) = call(close_kernel, [((LEVELS, TRACERS, CELLS), F32)], to_depth(value), wet)
    return adjoint


def solution(mesh):
    return jax.shard_map(
        local,
        mesh=mesh,
        in_specs=(
            P("depth", None, "region"),
            P("region"),
            P("depth", "region", None),
            P("depth", "region"),
            P("depth", "region"),
            P("depth", "region"),
            P("depth", "region"),
            P("depth", "region", None),
            P("depth", "region"),
            P("depth", "region"),
            P("depth", "region"),
        ),
        out_specs=P("depth", None, "region"),
        check_vma=False,
    )
```

```python
import jax
import jax.numpy as jnp
from jax import lax
from jax.experimental import pallas as pl
from jax.experimental.pallas import tpu as pltpu
from jax.sharding import PartitionSpec as P

STEPS = 12
LEVEL_STEPS = 4
GROUPS = 8
PAIR = 2
LEVELS = 8
TRACERS = GROUPS * PAIR
CELLS = 128
STATE = 128
LISTS = 16
BF = jnp.bfloat16
F32 = jnp.float32
I32 = jnp.int32


def dot(a, b):
    return jnp.dot(a, b, preferred_element_type=F32)


def dot_last(a, b):
    return lax.dot_general(a, b, (((1,), (1,)), ((), ())), preferred_element_type=F32)


def iota(shape, dim):
    return lax.broadcasted_iota(I32, shape, dim)


def spread(codes, slots, rows):
    owner = (iota((slots * rows, CELLS), 0) // rows == iota((slots * rows, CELLS), 1)).astype(BF)
    return dot_last(owner, codes).astype(I32), dot_last(codes, owner).astype(I32)


def write_picks(wanted, rows, left, right, part=slice(None)):
    count = wanted.shape[0]
    hit = jnp.where(wanted == iota((count, STATE), 1), 1.0, 0.0)
    even = iota((count, STATE), 0) // rows % 2 == 0
    left[part] = jnp.where(even, hit, 0.0).astype(BF)
    right[part] = jnp.where(even, 0.0, hit).astype(BF)


def write_place(wanted, place, part=slice(None)):
    shape = (place.shape[0], wanted.shape[1])
    place[:, part] = jnp.where(wanted == iota(shape, 0), 1.0, 0.0).astype(BF)


def level_matrices(codes, row_of, block_of, slots, left, right, place):
    columns, rows = spread(codes, slots, TRACERS)
    tracer = iota((slots * TRACERS, 1), 0) % TRACERS
    wanted = tracer // PAIR * TRACERS + columns[:, row_of : row_of + 1] * PAIR + tracer % PAIR
    write_picks(wanted, TRACERS, left, right)
    tracer = iota((1, slots * TRACERS), 1) % TRACERS
    block = rows[block_of : block_of + 1]
    wanted = block // LEVELS * STATE + tracer // PAIR * TRACERS + block % LEVELS * PAIR + tracer % PAIR
    write_place(jnp.where(block < 0, -1, wanted), place)


def level_products(rows, left, right, place, tiles):
    rows = rows.astype(BF)
    x_left = dot(left[...], rows).astype(BF)
    x_right = dot(right[...], rows).astype(BF)
    parts = []
    for at in range(0, tiles.shape[0], 4):
        part = slice(at * TRACERS, (at + 4) * TRACERS)
        lhs = jnp.concatenate([x_left[part], x_right[part]], axis=1)
        upper = jnp.concatenate([tiles[at], tiles[at + 2]], axis=1)
        lower = jnp.concatenate([tiles[at + 1], tiles[at + 3]], axis=1)
        out = dot(lhs, jnp.concatenate([upper, lower], axis=0))
        parts += [out[: 2 * TRACERS, :CELLS], out[2 * TRACERS :, CELLS:]]
    return placed(place, jnp.concatenate(parts, axis=0))


def placed(place, product):
    return dot(place[...], product.astype(BF))


def open_kernel(
    seed, lengths, l_rows, l_sides, l_targets, l_count, v_rows, v_peers, v_targets, tiles,
    adjoint, partial, wet, left, right, place, codes,
):
    l_slots, v_slots = l_rows.shape[1], v_rows.shape[1]
    codes[...] = jnp.zeros(codes.shape, F32)
    odd = lax.axis_index("region") % 2
    side = jnp.where(odd == 1, 2 - l_sides[...], l_sides[...])
    used = iota((1, l_slots), 1) < l_count[...]
    codes[0:1, 0:l_slots] = l_rows[...].astype(F32)
    codes[1:2, 0:l_slots] = jnp.where(used, side * LEVELS + l_targets[...], -1).astype(F32)
    codes[2:3, 0:v_slots] = v_rows[...].astype(F32)
    codes[3:4, 0:v_slots] = (v_peers[...] * LEVELS + v_targets[...]).astype(F32)
    level = lax.axis_index("depth") * LEVELS + iota((STATE, CELLS), 0) % TRACERS // PAIR
    wet[...] = jnp.where(level < lengths[...], 1.0, 0.0)
    level_matrices(codes[...].astype(BF)[:8], 2, 3, v_slots, left, right, place)
    for group in range(GROUPS):
        for at in range(LEVELS):
            row = group * TRACERS + at * PAIR
            adjoint[row : row + PAIR] = seed[at, group * PAIR : group * PAIR + PAIR]
    value = wet[...] * adjoint[...]
    adjoint[...] = value
    sums = level_products(value, left, right, place, tiles).astype(BF)
    for peer in range(GROUPS):
        at = peer * (STATE + LISTS)
        partial[at : at + STATE] = sums[peer * STATE : (peer + 1) * STATE]
        partial[at + STATE : at + STATE + LISTS] = codes[...].astype(BF)


def lateral_lists_kernel(codes, left, right, place):
    level_matrices(codes[...].astype(BF)[:8], 0, 1, left.shape[0] // TRACERS, left, right, place)


def vertical_kernel(base, first, second, wet, left, right, place, tiles, adjoint, partial):
    value = wet[...] * (base[...] + first[...].astype(F32) + second[...].astype(F32))
    adjoint[...] = value
    partial[...] = level_products(value, left, right, place, tiles).astype(BF)


def lateral_kernel(adjoint, returned, wet, left, right, place, tiles, base, to_first, to_second):
    value = adjoint[...]
    stride = returned.shape[0] // GROUPS
    for peer in range(GROUPS):
        value = value + returned[stride * peer : stride * peer + STATE].astype(F32)
    value = wet[...] * value
    partial = level_products(value, left, right, place, tiles).astype(BF)
    to_first[...] = partial[:STATE]
    to_second[...] = partial[2 * STATE :]
    base[...] = value + partial[STATE : 2 * STATE].astype(F32)


def tracer_lists_kernel(returned, lengths, wet, v_left, v_right, v_place, l_left, l_right, l_place, lines_l, lines_v):
    level = iota((STATE, CELLS), 0) // PAIR
    wet[...] = jnp.where(level < lengths[...], 1.0, 0.0)
    l_rows, v_rows = l_left.shape[0] // GROUPS, v_left.shape[0] // GROUPS
    stride = STATE + LISTS
    for depth in range(GROUPS):
        codes = returned[depth * stride + STATE : (depth + 1) * stride][:8]
        for rows, row_of, left, right in ((l_rows, 0, l_left, l_right), (v_rows, 2, v_left, v_right)):
            columns, lines = spread(codes, rows // PAIR, PAIR)
            part = slice(depth * rows, (depth + 1) * rows)
            wanted = (depth * LEVELS + columns[:, row_of : row_of + 1]) * PAIR + iota((rows, 1), 0) % PAIR
            write_picks(wanted, PAIR, left, right, part)
            block = lines[row_of + 1 : row_of + 2]
            pair = iota((1, rows), 1) % PAIR
            if row_of == 0:
                wanted = block // LEVELS * STATE + (depth * LEVELS + block % LEVELS) * PAIR + pair
                wanted = jnp.where(block < 0, -1, wanted)
            else:
                wanted = block * PAIR + pair
            line = lines_l if row_of == 0 else lines_v
            line[:, part] = jnp.broadcast_to(wanted, (8, rows))
    write_place(lines_l[0:1], l_place)
    write_place(lines_v[0:1], v_place)


def tracer_products(rows, left, right, place, tiles, first, slots, scratch):
    x_left, x_right, product = scratch
    count = left.shape[0]
    rows = rows.astype(BF)
    x_left[:count] = dot(left[...], rows).astype(BF)
    x_right[:count] = dot(right[...], rows).astype(BF)
    upper_rows = iota((8, CELLS), 0) < 2 * PAIR
    blocks = tiles.shape[0] // GROUPS
    for depth in range(GROUPS):
        for octet in range(slots // 8):
            at = (depth * slots + octet * 8) * PAIR
            part = slice(at, at + 8 * PAIR)
            lhs = jnp.concatenate([x_left[part], x_right[part]], axis=1)
            for quad in range(2):
                tile = depth * blocks + first + octet * 8 + quad * 4
                upper = jnp.concatenate([tiles[tile], tiles[tile + 2]], axis=1)
                lower = jnp.concatenate([tiles[tile + 1], tiles[tile + 3]], axis=1)
                out = dot(lhs, jnp.concatenate([upper, lower], axis=0))[8 * quad : 8 * quad + 8]
                product[at + 8 * quad : at + 8 * quad + 8] = jnp.where(upper_rows, out[:, :CELLS], out[:, CELLS:])
    return placed(place, product[:count])


def tracer_step(value, wet, v_left, v_right, v_place, l_left, l_right, l_place, tiles, base, to_first, to_second, *scratch):
    l_slots, v_slots = l_left.shape[0] // (GROUPS * PAIR), v_left.shape[0] // (GROUPS * PAIR)
    value = wet[...] * value
    value = wet[...] * (value + tracer_products(value, v_left, v_right, v_place, tiles, l_slots, v_slots, scratch))
    partial = tracer_products(value, l_left, l_right, l_place, tiles, 0, l_slots, scratch)
    to_first[...] = partial[:STATE].astype(BF)
    to_second[...] = partial[2 * STATE :].astype(BF)
    base[...] = value + partial[STATE : 2 * STATE]


def tracer_first_kernel(value, *refs):
    tracer_step(value[...], *refs)


def tracer_kernel(base, first, second, *refs):
    tracer_step(base[...] + first[...].astype(F32) + second[...].astype(F32), *refs)


def sum_kernel(base, first, second, total):
    total[...] = base[...] + first[...].astype(F32) + second[...].astype(F32)


def close_kernel(value, wet, out):
    rows = wet[...] * value[...]
    for group in range(GROUPS):
        for at in range(LEVELS):
            row = group * TRACERS + at * PAIR
            out[at, group * PAIR : group * PAIR + PAIR] = rows[row : row + PAIR]


def call(body, outs, *args, scratch=()):
    return pl.pallas_call(
        body,
        out_shape=[jax.ShapeDtypeStruct(shape, kind) for shape, kind in outs],
        in_specs=[pl.BlockSpec(memory_space=pltpu.VMEM) for _ in args],
        out_specs=[pl.BlockSpec(memory_space=pltpu.VMEM) for _ in outs],
        scratch_shapes=scratch,
        compiler_params=pltpu.CompilerParams(vmem_limit_bytes=24 * 1024 * 1024),
    )(*args)


def swapped(to_first, to_second):
    regions = lax.axis_size("region")
    first = [(i, (i + 1) % regions if i % 2 else (i - 1) % regions) for i in range(regions)]
    second = [(i, i ^ 1) for i in range(regions)]
    from_first = lax.ppermute(to_first, "region", first)
    from_second = lax.ppermute(to_second, "region", second)
    return from_first, from_second


def to_depth(value):
    return lax.all_to_all(value, "depth", split_axis=0, concat_axis=0, tiled=True)


def local(
    adjoint_seed,
    column_lengths,
    lateral_tiles,
    lateral_rows,
    lateral_sides,
    lateral_targets,
    lateral_counts,
    vertical_tiles,
    vertical_rows,
    vertical_peers,
    vertical_targets,
):
    gathered = lax.all_gather(
        jnp.concatenate([lateral_tiles, vertical_tiles], axis=0), "depth", axis=0, tiled=True
    )
    l_slots, v_slots = lateral_tiles.shape[0], vertical_tiles.shape[0]
    lengths = column_lengths.reshape(1, CELLS)
    state = ((STATE, CELLS), F32)
    sent = ((STATE, CELLS), BF)

    def matrices(slots, blocks):
        return [((slots * TRACERS, STATE), BF)] * 2 + [((blocks * STATE, slots * TRACERS), BF)]

    adjoint, partial, wet, *vertical, codes = call(
        open_kernel,
        [state, ((GROUPS * (STATE + LISTS), CELLS), BF), state]
        + matrices(v_slots, GROUPS)
        + [((LISTS, CELLS), F32)],
        adjoint_seed,
        lengths,
        lateral_rows.reshape(1, l_slots),
        lateral_sides.reshape(1, l_slots),
        lateral_targets.reshape(1, l_slots),
        lateral_counts,
        vertical_rows.reshape(1, v_slots),
        vertical_peers.reshape(1, v_slots),
        vertical_targets.reshape(1, v_slots),
        vertical_tiles,
    )
    lateral = call(lateral_lists_kernel, matrices(l_slots, 3), codes)
    returned = first_returned = to_depth(partial)
    for step in range(LEVEL_STEPS):
        base, to_first, to_second = call(
            lateral_kernel, [state, sent, sent], adjoint, returned, wet, *lateral, lateral_tiles
        )
        received = swapped(to_first, to_second)
        if step < LEVEL_STEPS - 1:
            adjoint, partial = call(
                vertical_kernel,
                [state, ((GROUPS * STATE, CELLS), BF)],
                base,
                *received,
                wet,
                *vertical,
                vertical_tiles,
            )
            returned = to_depth(partial)

    def tracer_matrices(slots, blocks):
        rows = slots * PAIR
        return [((GROUPS * rows, STATE), BF)] * 2 + [((blocks * STATE, GROUPS * rows), BF)]

    constants = call(
        tracer_lists_kernel,
        [state] + tracer_matrices(v_slots, 1) + tracer_matrices(l_slots, 3),
        first_returned,
        lengths,
        scratch=[pltpu.VMEM((8, GROUPS * slots * PAIR), I32) for slots in (l_slots, v_slots)],
    )
    rows = GROUPS * l_slots * PAIR
    scratch = [pltpu.VMEM((rows, CELLS), kind) for kind in (BF, BF, F32)]
    (value,) = call(sum_kernel, [state], base, *received)
    value = to_depth(value)
    for step in range(LEVEL_STEPS, STEPS):
        if step == LEVEL_STEPS:
            arrived, body = (value,), tracer_first_kernel
        else:
            arrived, body = (base, *received), tracer_kernel
        base, to_first, to_second = call(body, [state, sent, sent], *arrived, *constants, gathered, scratch=scratch)
        received = swapped(to_first, to_second)
    (value,) = call(sum_kernel, [state], base, *received)
    (adjoint,) = call(close_kernel, [((LEVELS, TRACERS, CELLS), F32)], to_depth(value), wet)
    return adjoint


def solution(mesh):
    return jax.shard_map(
        local,
        mesh=mesh,
        in_specs=(
            P("depth", None, "region"),
            P("region"),
            P("depth", "region", None),
            P("depth", "region"),
            P("depth", "region"),
            P("depth", "region"),
            P("depth", "region"),
            P("depth", "region", None),
            P("depth", "region"),
            P("depth", "region"),
            P("depth", "region"),
        ),
        out_specs=P("depth", None, "region"),
        check_vma=False,
    )
```
